512 devices in a mesh: dp: 32 (over x, y), tensor: 16 (over z, core).
Axes of the slice: x: 4, y: 8, z: 8, core: 2. Of those that a mesh axis runs over, the one named last changes fastest.
Arguments:
- gradient: bfloat16 [24, 512, 512], P(None, 'dp', 'tensor'), may hold values from -6 to 6
- weight: bfloat16 [24, 512, 512], P(None, 'dp', 'tensor'), may hold values from -0.625 to 0.625
- owner_map: int32 [24, 1], replicated, may hold values from 0 to 15; in each aligned block of 24 rows (0 to 23, 24 to 47, ...) at most 3 rows name the same one
- stored_left_eigenvectors: bfloat16 [48, 512, 512], P('tensor'), may hold values from -0.25 to 0.25
- stored_right_eigenvectors: bfloat16 [48, 512, 512], P('tensor'), may hold values from -0.25 to 0.25
- left_gram: float32 [48, 512, 512], P('tensor', 'dp'), may hold values from -1024 to 1024, as said below
- right_gram: float32 [48, 512, 512], P('tensor', 'dp'), may hold values from -1024 to 1024, as said below
- rotated_first_moment: float32 [48, 512, 512], P('tensor', 'dp'), may hold values from -1.75 to 1.75
- rotated_second_moment: float32 [48, 512, 512], P('tensor', 'dp'), may hold values from 0.02 to 1
Outputs:
- new_weight: bfloat16 [24, 512, 512], P(None, None, 'tensor')
- new_left_gram: float32 [48, 512, 512], P('tensor', 'dp')
- new_right_gram: float32 [48, 512, 512], P('tensor', 'dp')
- new_first_moment: float32 [48, 512, 512], P('tensor', 'dp')
- new_second_moment: float32 [48, 512, 512], P('tensor', 'dp')
The draws below stay inside these ranges and needn't reach their ends.
Inputs may be any that keep to these rules, and one draw needn't show every extreme that they name: `owner_map`: every tensor index owns at least one block and at most 3; some index owns exactly 3. `left_gram`: symmetric; diagonal entries between 256 and 1024. `right_gram`: symmetric; diagonal entries between 256 and 1024.
All inputs are finite; a program needn't handle non-finite values.
Results may differ from the reference program's by a relative error of at most 0.0021.
Values may be sent and summed in bfloat16 or wider, within the bound.
A program may use at most 64 MiB of HBM per device.

```python
import math
import jax
import jax.numpy as jnp
import numpy as np
from jax import lax

BLOCK_ORDER_SIZE = 512
SLOT = 3
NBLK = 24
STATE_SLOT_COUNT = 48
N_TENSOR = 16


def sample_gram_matrix(key, count, order):
    key_off, key_diag = jax.random.split(key)
    jitter = jax.random.truncated_normal(key_off, -4.0, 4.0, (count, order, order), jnp.float32)
    off_part = 0.2 * math.sqrt(order) * (jitter + jnp.swapaxes(jitter, 1, 2))
    log_level = jax.random.uniform(key_diag, (count, order, 1), jnp.float32, math.log(0.5), math.log(2.0))
    diag_part = order * jnp.exp(log_level)
    row_index = lax.broadcasted_iota(jnp.int32, (order, order), 0)
    col_index = lax.broadcasted_iota(jnp.int32, (order, order), 1)
    return jnp.where((row_index == col_index)[None], diag_part, off_part)


def draw_left_gram(key, part):
    key = jax.random.fold_in(key, 11)
    return sample_gram_matrix(key, STATE_SLOT_COUNT, BLOCK_ORDER_SIZE)


def draw_right_gram(key, part):
    key = jax.random.fold_in(key, 12)
    return sample_gram_matrix(key, STATE_SLOT_COUNT, BLOCK_ORDER_SIZE)


def level_of(rng, shape, pieces, low, largest):
    def one(dim, shards_of):
        draws = jax.random.uniform(jax.random.fold_in(jax.random.fold_in(rng, 6), dim), (shards_of,), jnp.float32, low / len(pieces), largest / len(pieces))
        return jnp.repeat(jnp.exp(draws), shape[dim] // shards_of).reshape((-1,) + (1,) * (len(shape) - dim - 1))

    gain = one(*pieces[0])
    for cut in pieces[1:]:
        gain = gain * one(*cut)
    return gain


def shared_out(rng, own, number, rows, number_of, top, limit, slope):
    ranking = jax.random.permutation(rng, number_of)
    heavy_load, common = portions_of(number_of, rows * top, limit, slope, True), portions_of(number_of, rows * top, limit, slope, False)
    places = jnp.arange(number_of)

    def named(sizes, rotation):
        used = int((sizes > 0).sum())
        fixed = max(1, used // 4)
        moved = fixed + (places - fixed + rotation * (used - fixed)) % max(1, number_of - fixed)
        return jnp.zeros((number_of,), jnp.int32).at[ranking[jnp.where(places < fixed, places, moved)]].set(jnp.asarray(sizes, jnp.int32))

    sizes = jnp.where(number % 4 == 0, named(heavy_load, number // 4), named(common, number - number // 4 - 1))
    mixed = jax.random.permutation(jax.random.fold_in(own, 3), number_of)
    giver, receiver = mixed[0:number_of // 2 * 2:2], mixed[1:number_of // 2 * 2:2]
    margin = jnp.minimum(sizes[giver] - 1, limit - sizes[receiver]) // 2
    margin = jnp.where((giver == ranking[0]) | (receiver == ranking[0]) | (sizes[receiver] == 0), 0, jnp.maximum(margin, 0))
    moved = jax.random.randint(jax.random.fold_in(own, 4), (number_of // 2,), 0, 1 << 20) % (margin + 1)
    sizes = sizes.at[giver].add(-moved).at[receiver].add(moved)
    items = jnp.searchsorted(jnp.cumsum(sizes), jnp.arange(rows * top), side="right").astype(jnp.int32)
    table = items.reshape(top, rows).T
    table = table[jax.random.permutation(jax.random.fold_in(own, 1), rows)]
    rotation = jax.random.randint(jax.random.fold_in(own, 2), (rows, 1), 0, top)
    return jnp.take_along_axis(table, (jnp.arange(top)[None, :] + rotation) % top, axis=1)


def portions_of(amount, total, reach, skew, full):
    weights = [(1 << 20) // math.isqrt(standing ** skew) + 1 for standing in range(1, amount + 1)]
    largest = reach if full else min(reach, max(-(-total // amount), total * weights[0] // sum(weights)))
    least = 1 if total - largest >= amount - 1 else 0
    holding, spare = [largest] + [least] * (amount - 1), total - largest - least * (amount - 1)
    while spare > 0:
        free = [i for i in range(1, amount) if holding[i] < largest] or [i for i in range(1, amount) if holding[i] < reach]
        mass, left = sum([weights[i] for i in free]), spare
        for i in free:
            extra = min(reach - holding[i], max(1, left * weights[i] // mass), spare)
            holding[i] = holding[i] + extra
            spare = spare - extra
    return np.array(holding)


def noise(stream_key, shape, scale, reach, pieces=(), kind=jnp.bfloat16):
    drawn = jax.random.normal(stream_key, shape, jnp.float32) * scale
    if len(pieces) > 0:
        drawn = level_of(stream_key, shape, pieces, -0.22, 0.18) * drawn
    return jnp.clip(drawn, min=-reach, max=reach).astype(kind)


def setup_inputs(seed: int = 0) -> dict:
    key_list = jax.random.split(jax.random.key(seed), 10)
    gradient = noise(key_list[0], (NBLK, BLOCK_ORDER_SIZE, BLOCK_ORDER_SIZE), 1.0, 6.0, ((1, 32), (2, 16)))
    weight = noise(key_list[1], (NBLK, BLOCK_ORDER_SIZE, BLOCK_ORDER_SIZE), 0.1, 0.625, ((1, 32), (2, 16)))
    owner_map_keys = jax.random.split(jax.random.fold_in(key_list[2], 1), NBLK // NBLK)
    owner_map_turns = jax.random.permutation(jax.random.fold_in(key_list[2], 3), NBLK // NBLK)
    owner_map = jax.vmap(lambda own, number: shared_out(jax.random.fold_in(key_list[2], 2), own, number, NBLK, N_TENSOR, 1, SLOT, 2))(owner_map_keys, owner_map_turns).reshape((NBLK, 1))
    stored_left_eigenvectors = noise(key_list[3], (STATE_SLOT_COUNT, BLOCK_ORDER_SIZE, BLOCK_ORDER_SIZE), BLOCK_ORDER_SIZE ** -0.5, 0.25, ((0, 16),))
    stored_right_eigenvectors = noise(key_list[4], (STATE_SLOT_COUNT, BLOCK_ORDER_SIZE, BLOCK_ORDER_SIZE), BLOCK_ORDER_SIZE ** -0.5, 0.25, ((0, 16),))
    left_gram = draw_left_gram(jax.random.fold_in(key_list[9], 71), 0)
    right_gram = draw_right_gram(jax.random.fold_in(key_list[9], 71), 0)
    rotated_first_moment = noise(key_list[7], (STATE_SLOT_COUNT, BLOCK_ORDER_SIZE, BLOCK_ORDER_SIZE), 0.3, 1.75, ((0, 16), (1, 32)), jnp.float32)
    rotated_second_moment = jnp.clip(jnp.exp(math.log(1.0) - 3.912023 * jax.random.uniform(key_list[8], (STATE_SLOT_COUNT, BLOCK_ORDER_SIZE, BLOCK_ORDER_SIZE), jnp.float32) ** level_of(key_list[8], (STATE_SLOT_COUNT, BLOCK_ORDER_SIZE, BLOCK_ORDER_SIZE), ((0, 16), (1, 32)), -0.2, 0.2)), 0.02, 1.0)
    return dict(gradient=gradient, weight=weight, owner_map=owner_map, stored_left_eigenvectors=stored_left_eigenvectors, stored_right_eigenvectors=stored_right_eigenvectors, left_gram=left_gram, right_gram=right_gram, rotated_first_moment=rotated_first_moment, rotated_second_moment=rotated_second_moment)


beta_one = 0.9
beta_two = 0.999
beta_gram = 0.95
epsilon = 1e-08
learn_rate = 0.01
decay_rate = 0.1

def slot_table(owner_map, slot_count, owners):
    owner_ids = owner_map[:, 0].astype(jnp.int32)
    blocks = owner_ids.shape[0]
    block_ids = jnp.arange(blocks, dtype=jnp.int32)
    before = block_ids[:, None] > block_ids[None, :]
    matches = owner_ids[:, None] == owner_ids[None, :]
    position = lax.optimization_barrier(jnp.sum(jnp.where(before & matches, 1, 0), axis=1)).astype(jnp.int32)
    target = owner_ids * slot_count + position
    slot_ids = jnp.arange(owners * slot_count, dtype=jnp.int32)
    return slot_ids[:, None] == target[None, :]

def update_slot(inputs):
    grad_block, left_q, right_q, gram_left, gram_right, moment_one, moment_two = inputs
    half_turn = jnp.dot(grad_block, right_q, preferred_element_type=jnp.float32).astype(jnp.bfloat16)
    rotated = jnp.dot(left_q.T, half_turn, preferred_element_type=jnp.float32)
    moment_one = beta_one * moment_one + (1.0 - beta_one) * rotated
    moment_two = beta_two * moment_two + (1.0 - beta_two) * rotated * rotated
    direction = (moment_one / (jnp.sqrt(moment_two) + epsilon)).astype(jnp.bfloat16)
    back_turn = jnp.dot(direction, right_q.T, preferred_element_type=jnp.float32).astype(jnp.bfloat16)
    update = jnp.dot(left_q, back_turn, preferred_element_type=jnp.float32).astype(jnp.bfloat16)
    gram_scale = 1.0 - beta_gram
    gram_left = beta_gram * gram_left + gram_scale * jnp.dot(grad_block, grad_block.T, preferred_element_type=jnp.float32)
    gram_right = beta_gram * gram_right + gram_scale * jnp.dot(grad_block.T, grad_block, preferred_element_type=jnp.float32)
    return (update, gram_left, gram_right, moment_one, moment_two)

def reference(gradient, weight, owner_map, stored_left_eigenvectors, stored_right_eigenvectors, left_gram, right_gram, rotated_first_moment, rotated_second_moment):
    one_hot = slot_table(owner_map, SLOT, N_TENSOR).astype(jnp.float32)
    packed = jnp.einsum('qb,bij->qij', one_hot, gradient.astype(jnp.float32)).astype(jnp.bfloat16)
    update, new_left, new_right, moment_one, moment_two = lax.map(update_slot, (packed, stored_left_eigenvectors, stored_right_eigenvectors, left_gram, right_gram, rotated_first_moment, rotated_second_moment))
    unpacked = jnp.einsum('qb,qij->bij', one_hot, update.astype(jnp.float32)).astype(jnp.bfloat16)
    weight_wide = weight.astype(jnp.float32)
    stepped = weight_wide - learn_rate * (unpacked.astype(jnp.float32) + decay_rate * weight_wide)
    return (stepped.astype(jnp.bfloat16), new_left, new_right, moment_one, moment_two)
```

```python
import jax
import jax.numpy as jnp
from jax import lax
from jax.experimental import pallas as pl
from jax.experimental.pallas import tpu as pltpu
from jax.sharding import PartitionSpec as P

beta_one = 0.9
beta_two = 0.999
beta_gram = 0.95
epsilon = 1e-08
learn_rate = 0.01
decay_rate = 0.1

MESH = pl.DeviceIdType.MESH
F32 = jnp.float32
BF16 = jnp.bfloat16

NX = 4
NY = 8
ND = NX * NY
NT = 16
NB = 24
NS = 3
N = 512
R = 16
C = 32


def dot_nt(a, b):
    return lax.dot_general(a, b, (((1,), (1,)), ((), ())), preferred_element_type=F32)


def dot_nn(a, b):
    return lax.dot_general(a, b, (((1,), (0,)), ((), ())), preferred_element_type=F32)


def ring_gather(buf, ssem, rsem, x, y):
    count = [0]
    started = []

    def place(dx, dy):
        return lax.rem(x + dx + NX, NX) * NY + lax.rem(y + dy + NY, NY)

    def send(flow, dx, dy, tx, ty):
        src = place(dx, dy)
        copy = pltpu.make_async_remote_copy(
            src_ref=buf.at[flow, src],
            dst_ref=buf.at[flow, src],
            send_sem=ssem.at[count[0]],
            recv_sem=rsem.at[flow, src],
            device_id={"dp": place(tx, ty)},
            device_id_type=MESH,
        )
        count[0] += 1
        copy.start()
        started.append(copy)

    def arrive(flow, dx, dy):
        src = place(dx, dy)
        pltpu.make_async_remote_copy(
            src_ref=buf.at[flow, src],
            dst_ref=buf.at[flow, src],
            send_sem=ssem.at[0],
            recv_sem=rsem.at[flow, src],
            device_id={"dp": place(1, 0)},
            device_id_type=MESH,
        ).wait_recv()

    events = []

    def add(time, flow, dx, dy, forwards):
        events.append((time, len(events), flow, dx, dy, forwards))

    legs = [(0, 0)] + [(-k, k) for k in range(1, 5)] + [(k, k) for k in range(1, 4)]
    for dy, time in legs:
        forwards = []
        if -3 <= dy <= 0:
            forwards.append((0, 1))
        if 0 <= dy <= 2:
            forwards.append((0, -1))
        forwards += [(1, 0), (-1, 0)]
        add(time, 0, 0, dy, forwards)
        right = dy in (-4, -2, 1, 3)
        add(time + 1, 0, -1, dy, [(1, 0)] if right else [])
        add(time + 1, 0, 1, dy, [] if right else [(-1, 0)])
        add(time + 2, 0, 2, dy, [])
    for dx, first in ((0, 0), (1, 1), (-1, 1), (2, 1.5)):
        up, down = (4, 3) if dx in (0, 2) else (3, 4)
        forwards = [(0, 1), (0, -1)]
        if dx == 0:
            forwards = [(1, 0), (-1, 0), (2, 0)] + forwards
        add(first, 1, dx, 0, forwards)
        for k in range(1, up + 1):
            add(first + k, 1, dx, -k, [(0, 1)] if k < up else [])
        for k in range(1, down + 1):
            add(first + k, 1, dx, k, [(0, -1)] if k < down else [])

    for time, _, flow, dx, dy, forwards in sorted(events):
        if dx != 0 or dy != 0:
            arrive(flow, dx, dy)
        for tx, ty in forwards:
            send(flow, dx, dy, tx, ty)
    return started


def kernel(
    own,
    grad,
    weight,
    ql_hbm,
    qr_hbm,
    lg_hbm,
    rg_hbm,
    m1_hbm,
    m2_hbm,
    out_w,
    nl_hbm,
    nr_hbm,
    nm1_hbm,
    nm2_hbm,
    ql,
    qr,
    lg,
    rg,
    m1,
    m2,
    wide,
    wrow,
    zsend,
    zrecv,
    gbuf,
    qlc,
    dpad,
    bsend,
    brecv,
    vpad,
    usend,
    urecv,
    ysend,
    yrecv,
    wbuf,
    lsem,
    osem,
    zssem,
    zrsem,
    gssem,
    grsem,
    bssem,
    brsem,
    ussem,
    ursem,
    yssem,
    yrsem,
    wrsem,
):
    d = lax.axis_index("dp")
    t = lax.axis_index("tensor")
    x = d // NY
    y = lax.rem(d, NY)

    barrier = pltpu.get_barrier_semaphore()
    for k in range(1, NT):
        pl.semaphore_signal(
            barrier, inc=1, device_id={"tensor": lax.rem(t + k, NT)}, device_id_type=MESH
        )
    for k in range(1, ND):
        pl.semaphore_signal(
            barrier, inc=1, device_id={"dp": lax.rem(d + k, ND)}, device_id_type=MESH
        )

    loads = []
    for i, (src, dst) in enumerate(
        ((ql_hbm, ql), (qr_hbm, qr), (m1_hbm, m1), (m2_hbm, m2), (lg_hbm, lg), (rg_hbm, rg))
    ):
        copy = pltpu.make_async_copy(src, dst, lsem.at[i])
        copy.start()
        loads.append(copy)

    owner = [own[b] for b in range(NB)]
    position = []
    for b in range(NB):
        before = jnp.int32(0)
        for b2 in range(b):
            before = before + (owner[b2] == owner[b]).astype(jnp.int32)
        position.append(before)

    lane = lax.broadcasted_iota(jnp.int32, (C, 128), 1)
    row = lax.broadcasted_iota(jnp.int32, (C, 128), 0)
    repeat = jnp.where(lax.rem(lane, C) == row, 1.0, 0.0).astype(BF16)
    wide[...] = dot_nn(grad[...].reshape(NB * R, C), repeat)
    group32 = lax.broadcasted_iota(jnp.int32, (R, 128), 1) // 32
    group16 = lax.broadcasted_iota(jnp.int32, (R, 128), 1) // 16
    zero = jnp.zeros((R, 128), F32)

    u = lax.rem(t, 4)
    place = [lax.rem(u + position[b], 4) for b in range(NB)]
    for o in range(NT):
        tile = zero
        for b in range(NB):
            chosen = jnp.where(owner[b] == o, place[b], -1)
            tile = jnp.where(group32 == chosen, wide[b * R : (b + 1) * R, :], tile)
        zsend[o] = tile.astype(BF16)

    pl.semaphore_wait(barrier, NT - 1 + ND - 1)

    zcopies = []
    for k in range(1, NT):
        o = lax.rem(t + k, NT)
        copy = pltpu.make_async_remote_copy(
            src_ref=zsend.at[o],
            dst_ref=zrecv.at[t],
            send_sem=zssem.at[k],
            recv_sem=zrsem.at[t],
            device_id={"tensor": o},
            device_id_type=MESH,
        )
        copy.start()
        zcopies.append(copy)
    zrecv[t] = zsend[t]

    wwide = dot_nn(weight[...].reshape(NB * R, C), repeat)
    for k in range(NB // 4):
        tile = zero
        for j in range(4):
            b = 4 * k + j
            tile = jnp.where(group32 == j, wwide[b * R : (b + 1) * R, :], tile)
        wrow[:, 128 * k : 128 * (k + 1)] = tile
    for s in range(NS):
        dpad[s] = jnp.zeros((128, N), BF16)
        vpad[s] = jnp.zeros((128, N), BF16)

    for k in range(1, NT):
        o = lax.rem(t + k, NT)
        pltpu.make_async_remote_copy(
            src_ref=zsend.at[o],
            dst_ref=zrecv.at[o],
            send_sem=zssem.at[k],
            recv_sem=zrsem.at[o],
            device_id={"tensor": o},
            device_id_type=MESH,
        ).wait_recv()

    for k in range(4):
        tiles = [zrecv[4 * k + j].astype(F32) for j in range(4)]
        for s in range(NS):
            tile = zero
            for j in range(4):
                tile = jnp.where(group32 == (j + s) % 4, tiles[j], tile)
            if s:
                tile = pltpu.roll(tile, 128 - 32 * s, 1)
            gbuf[k // 2, d, s, :, 128 * (k % 2) : 128 * (k % 2 + 1)] = tile.astype(BF16)

    gcopies = ring_gather(gbuf, gssem, grsem, x, y)

    m = lax.rem(d, 8)
    tile_start = pl.multiple_of(128 * (d // 8), 128)
    pick = jnp.where(
        lax.broadcasted_iota(jnp.int32, (R, 128), 1)
        == lax.broadcasted_iota(jnp.int32, (R, 128), 0) + 16 * m,
        1.0,
        0.0,
    ).astype(BF16)
    loads[0].wait()
    for s in range(NS):
        qlc[s] = dot_nt(pick, ql[s, :, pl.ds(tile_start, 128)]).astype(BF16)

    def whole(flow, s):
        return gbuf[flow, :, s].reshape(N, N // 2)

    for i in range(1, 4):
        loads[i].wait()
    stores = []
    for s in range(NS):
        turned = jnp.concatenate([dot_nn(qlc[s], whole(f, s)) for f in range(2)], axis=1)
        high = turned.astype(BF16)
        low = (turned - high.astype(F32)).astype(BF16)
        both = dot_nn(jnp.concatenate([high, low], axis=0), qr[s])
        rotated = both[:R] + both[R:]
        first = beta_one * m1[s] + (1.0 - beta_one) * rotated
        second = beta_two * m2[s] + (1.0 - beta_two) * rotated * rotated
        m1[s] = first
        m2[s] = second
        direction = (first / (jnp.sqrt(second) + epsilon)).astype(BF16)
        at = pl.multiple_of(16 * lax.rem(m + s, 8), 16)
        dpad[s, pl.ds(at, 16), :] = direction
    for i, (src, dst) in enumerate(((m1, nm1_hbm), (m2, nm2_hbm))):
        copy = pltpu.make_async_copy(src, dst, osem.at[i])
        copy.start()
        stores.append(copy)

    turned = dot_nt(qr[0], dpad[0])
    for s in range(1, NS):
        turned = turned + dot_nt(qr[s], dpad[s])
    bsend[...] = turned.astype(BF16).reshape(ND, R, 128)

    def exchange(src, dst, ssem, rsem):
        copies = []
        for dx in (2, 1, 3, 0):
            for dy in (4, 3, 5, 2, 6, 1, 7, 0):
                if dx == 0 and dy == 0:
                    continue
                k = dx * NY + dy
                to = lax.rem(x + dx, NX) * NY + lax.rem(y + dy, NY)
                copy = pltpu.make_async_remote_copy(
                    src_ref=src.at[to],
                    dst_ref=dst.at[d],
                    send_sem=ssem.at[k],
                    recv_sem=rsem.at[d],
                    device_id={"dp": to},
                    device_id_type=MESH,
                )
                copy.start()
                copies.append(copy)
        dst[d] = src[d]
        return copies

    def received(src, dst, ssem, rsem):
        for k in range(1, ND):
            o = lax.rem(d + k, ND)
            pltpu.make_async_remote_copy(
                src_ref=src.at[o],
                dst_ref=dst.at[o],
                send_sem=ssem.at[k],
                recv_sem=rsem.at[o],
                device_id={"dp": o},
                device_id_type=MESH,
            ).wait_recv()

    bcopies = exchange(bsend, brecv, bssem, brsem)

    gram_scale = 1.0 - beta_gram
    loads[4].wait()
    for s in range(NS):
        mine = [gbuf[f, d, s] for f in range(2)]
        product = dot_nt(mine[0], whole(0, s)) + dot_nt(mine[1], whole(1, s))
        lg[s] = beta_gram * lg[s] + gram_scale * product
    copy = pltpu.make_async_copy(lg, nl_hbm, osem.at[2])
    copy.start()
    stores.append(copy)

    received(bsend, brecv, bssem, brsem)

    h = lax.rem(d, 2)
    for k in range(4):
        tiles = [brecv[8 * k + j].astype(F32) for j in range(8)]
        for s in range(NS):
            tile = zero
            for j in range(8):
                tile = jnp.where(group16 == (j + s) % 8, tiles[j], tile)
            if s:
                tile = pltpu.roll(tile, 128 - 16 * s, 1)
            at = pl.multiple_of(32 * s + 16 * h, 16)
            vpad[s, pl.ds(at, 16), 128 * k : 128 * (k + 1)] = tile.astype(BF16)
    update = dot_nt(ql[0], vpad[0])
    for s in range(1, NS):
        update = update + dot_nt(ql[s], vpad[s])
    usend[...] = update.astype(BF16).reshape(ND, R, 128)
    ucopies = exchange(usend, urecv, ussem, ursem)

    loads[5].wait()
    flow = d // 16
    within = pl.multiple_of(128 * lax.rem(d // 8, 2), 128)
    for s in range(NS):
        part = gbuf[flow, :, s, :, pl.ds(within, 128)].reshape(N, 128)
        columns = dot_nt(pick, part).astype(BF16)
        product = jnp.concatenate([dot_nn(columns, whole(f, s)) for f in range(2)], axis=1)
        rg[s] = beta_gram * rg[s] + gram_scale * product
    copy = pltpu.make_async_copy(rg, nr_hbm, osem.at[3])
    copy.start()
    stores.append(copy)

    received(usend, urecv, ussem, ursem)

    for o in range(NT):
        ysend[o] = (urecv[2 * o].astype(F32) + urecv[2 * o + 1].astype(F32)).astype(BF16)
    ycopies = []
    for k in range(1, NT):
        o = lax.rem(t + k, NT)
        copy = pltpu.make_async_remote_copy(
            src_ref=ysend.at[o],
            dst_ref=yrecv.at[t],
            send_sem=yssem.at[k],
            recv_sem=yrsem.at[t],
            device_id={"tensor": o},
            device_id_type=MESH,
        )
        copy.start()
        ycopies.append(copy)
    yrecv[t] = ysend[t]
    for copy in gcopies:
        copy.wait_send()
    for k in range(1, NT):
        o = lax.rem(t + k, NT)
        pltpu.make_async_remote_copy(
            src_ref=ysend.at[o],
            dst_ref=yrecv.at[o],
            send_sem=yssem.at[k],
            recv_sem=yrsem.at[o],
            device_id={"tensor": o},
            device_id_type=MESH,
        ).wait_recv()

    for k in range(NB // 4):
        tile = zero
        for j in range(4):
            b = 4 * k + j
            moved = pltpu.roll(
                yrecv[owner[b]].astype(F32), lax.rem(j - position[b] + 4, 4) * 32, 1
            )
            tile = jnp.where(group32 == j, moved, tile)
        old = wrow[:, 128 * k : 128 * (k + 1)]
        new = old - learn_rate * (tile + decay_rate * old)
        wbuf[k // 3, d, :, 128 * (k % 3) : 128 * (k % 3 + 1)] = new.astype(BF16)

    wcopies = ring_gather(wbuf, gssem, wrsem, x, y)

    eye = jnp.where(
        lax.broadcasted_iota(jnp.int32, (128, 128), 0)
        == lax.broadcasted_iota(jnp.int32, (128, 128), 1),
        1.0,
        0.0,
    ).astype(BF16)
    for k in range(NB // 4):
        part = wbuf[k // 3, :, :, 128 * (k % 3) : 128 * (k % 3 + 1)].reshape(N, 128)
        out_w[128 * k : 128 * (k + 1), :] = dot_nt(eye, part).astype(BF16)

    for copy in zcopies + bcopies + ucopies + ycopies + wcopies:
        copy.wait_send()
    for copy in stores:
        copy.wait()


def per_device(gradient, weight, owner_map, ql, qr, lg, rg, m1, m2):
    vmem = pl.BlockSpec(memory_space=pltpu.VMEM)
    anywhere = pl.BlockSpec(memory_space=pl.ANY)
    rows = jax.ShapeDtypeStruct((NS, R, N), F32)
    dma = pltpu.SemaphoreType.DMA
    outs = pl.pallas_call(
        kernel,
        out_shape=(jax.ShapeDtypeStruct((NB * C, N), BF16), rows, rows, rows, rows),
        in_specs=[pl.BlockSpec(memory_space=pltpu.SMEM), vmem, vmem] + [anywhere] * 6,
        out_specs=(vmem, anywhere, anywhere, anywhere, anywhere),
        scratch_shapes=[
            pltpu.VMEM((NS, N, N), BF16),
            pltpu.VMEM((NS, N, N), BF16),
            pltpu.VMEM((NS, R, N), F32),
            pltpu.VMEM((NS, R, N), F32),
            pltpu.VMEM((NS, R, N), F32),
            pltpu.VMEM((NS, R, N), F32),
            pltpu.VMEM((NB * R, 128), F32),
            pltpu.VMEM((R, NB * C), F32),
            pltpu.VMEM((NT, R, 128), BF16),
            pltpu.VMEM((NT, R, 128), BF16),
            pltpu.VMEM((2, ND, NS, R, N // 2), BF16),
            pltpu.VMEM((NS, R, N), BF16),
            pltpu.VMEM((NS, 128, N), BF16),
            pltpu.VMEM((ND, R, 128), BF16),
            pltpu.VMEM((ND, R, 128), BF16),
            pltpu.VMEM((NS, 128, N), BF16),
            pltpu.VMEM((ND, R, 128), BF16),
            pltpu.VMEM((ND, R, 128), BF16),
            pltpu.VMEM((NT, R, 128), BF16),
            pltpu.VMEM((NT, R, 128), BF16),
            pltpu.VMEM((2, ND, R, NB * C // 2), BF16),
            dma((6,)),
            dma((4,)),
            dma((NT,)),
            dma((NT,)),
            dma((62,)),
            dma((2, ND)),
            dma((ND,)),
            dma((ND,)),
            dma((ND,)),
            dma((ND,)),
            dma((NT,)),
            dma((NT,)),
            dma((2, ND)),
        ],
        compiler_params=pltpu.CompilerParams(
            collective_id=0, has_side_effects=True, vmem_limit_bytes=32 * 1024 * 1024
        ),
        name="soap_step",
    )(owner_map.reshape(NB), gradient, weight, ql, qr, lg, rg, m1, m2)
    new_weight = jnp.transpose(outs[0].reshape(NB, C, N), (0, 2, 1))
    return (new_weight,) + tuple(outs[1:])


def solution(mesh):
    in_specs = (
        P(None, "dp", "tensor"),
        P(None, "dp", "tensor"),
        P(),
        P("tensor", None, None),
        P("tensor", None, None),
        P("tensor", "dp", None),
        P("tensor", "dp", None),
        P("tensor", "dp", None),
        P("tensor", "dp", None),
    )
    out_specs = (
        P(None, None, "tensor"),
        P("tensor", "dp", None),
        P("tensor", "dp", None),
        P("tensor", "dp", None),
        P("tensor", "dp", None),
    )
    return jax.shard_map(
        per_device, mesh=mesh, in_specs=in_specs, out_specs=out_specs, check_vma=False
    )
```

```python
import jax
import jax.numpy as jnp
from jax import lax
from jax.experimental import pallas as pl
from jax.experimental.pallas import tpu as pltpu
from jax.sharding import PartitionSpec as P

beta_one = 0.9
beta_two = 0.999
beta_gram = 0.95
epsilon = 1e-08
learn_rate = 0.01
decay_rate = 0.1

MESH = pl.DeviceIdType.MESH
F32 = jnp.float32
BF16 = jnp.bfloat16

NX = 4
NY = 8
ND = NX * NY
NT = 16
NB = 24
NS = 3
N = 512
R = 16
C = 32
VMEM_LIMIT = 56 * 1024 * 1024


def dot_nt(a, b):
    return lax.dot_general(a, b, (((1,), (1,)), ((), ())), preferred_element_type=F32)


def dot_nn(a, b):
    return lax.dot_general(a, b, (((1,), (0,)), ((), ())), preferred_element_type=F32)


class PlaneGather:
    legs = (1, -1, 2, -2, 3, -3, 4)

    def __init__(self, buf, ssem, rsem, x, y):
        self.buf, self.ssem, self.rsem, self.x, self.y = buf, ssem, rsem, x, y
        self.started = []

    def place(self, dx, dy):
        return lax.rem(self.x + dx + NX, NX) * NY + lax.rem(self.y + dy + NY, NY)

    def copy_of(self, dx, dy, tx, ty):
        src = self.place(dx, dy)
        return pltpu.make_async_remote_copy(
            src_ref=self.buf.at[src],
            dst_ref=self.buf.at[src],
            send_sem=self.ssem.at[len(self.started)],
            recv_sem=self.rsem.at[src],
            device_id={"dp": self.place(tx, ty)},
            device_id_type=MESH,
        )

    def send(self, dx, dy, tx, ty):
        copy = self.copy_of(dx, dy, tx, ty)
        copy.start()
        self.started.append(copy)

    def arrive(self, dx, dy):
        src = self.place(dx, dy)
        pltpu.make_async_remote_copy(
            src_ref=self.buf.at[src],
            dst_ref=self.buf.at[src],
            send_sem=self.ssem.at[0],
            recv_sem=self.rsem.at[src],
            device_id={"dp": self.place(1, 0)},
            device_id_type=MESH,
        ).wait_recv()

    def along_y(self):
        for dy in self.legs:
            self.send(0, 0, 0, dy)

    def along_x(self, i):
        dy = 0
        if i > 0:
            dy = -self.legs[i - 1]
            self.arrive(0, dy)
        self.send(0, dy, 1, 0)
        self.send(0, dy, -1, 0)

    def onward(self, i):
        dy = 0 if i == 0 else -self.legs[i - 1]
        self.arrive(-1, dy)
        self.arrive(1, dy)
        if i % 2 == 0:
            self.send(-1, dy, 1, 0)
        else:
            self.send(1, dy, -1, 0)

    def last(self):
        for dy in (0,) + tuple(-k for k in self.legs):
            self.arrive(2, dy)


def kernel(
    own,
    grad,
    weight,
    ql_hbm,
    qr_hbm,
    lg_hbm,
    rg_hbm,
    m1_hbm,
    m2_hbm,
    w_hbm,
    nl_hbm,
    nr_hbm,
    nm1_hbm,
    nm2_hbm,
    out_w,
    ql,
    qr,
    lg,
    rg,
    m1,
    m2,
    wide,
    wrow,
    zsend,
    zrecv,
    gbuf,
    tall,
    hsend,
    hrecv,
    rsend,
    rrecv,
    dpad,
    bsend,
    brecv,
    vpad,
    usend,
    urecv,
    ysend,
    yrecv,
    wbuf,
    lsem,
    osem,
    zssem,
    zrsem,
    gssem,
    grsem,
    hssem,
    hrsem,
    rssem,
    rrsem,
    bssem,
    brsem,
    ussem,
    ursem,
    yssem,
    yrsem,
    wssem,
    wrsem,
):
    d = lax.axis_index("dp")
    t = lax.axis_index("tensor")
    x = d // NY
    y = lax.rem(d, NY)

    barrier = pltpu.get_barrier_semaphore()
    for k in range(1, NT):
        pl.semaphore_signal(
            barrier, inc=1, device_id={"tensor": lax.rem(t + k, NT)}, device_id_type=MESH
        )
    for k in range(1, ND):
        pl.semaphore_signal(
            barrier, inc=1, device_id={"dp": lax.rem(d + k, ND)}, device_id_type=MESH
        )

    def exchange(src, dst, ssem, rsem):
        copies = []
        for dx in (2, 1, 3, 0):
            for dy in (4, 3, 5, 2, 6, 1, 7, 0):
                if dx == 0 and dy == 0:
                    continue
                k = dx * NY + dy
                to = lax.rem(x + dx, NX) * NY + lax.rem(y + dy, NY)
                copy = pltpu.make_async_remote_copy(
                    src_ref=src.at[to],
                    dst_ref=dst.at[d],
                    send_sem=ssem.at[k],
                    recv_sem=rsem.at[d],
                    device_id={"dp": to},
                    device_id_type=MESH,
                )
                copy.start()
                copies.append(copy)
        dst[d] = src[d]
        return copies

    def received(src, dst, ssem, rsem):
        for k in range(1, ND):
            o = lax.rem(d + k, ND)
            pltpu.make_async_remote_copy(
                src_ref=src.at[o],
                dst_ref=dst.at[o],
                send_sem=ssem.at[k],
                recv_sem=rsem.at[o],
                device_id={"dp": o},
                device_id_type=MESH,
            ).wait_recv()

    loads = []
    for i, (src, dst) in enumerate(
        ((ql_hbm, ql), (qr_hbm, qr), (m1_hbm, m1), (m2_hbm, m2), (lg_hbm, lg), (rg_hbm, rg))
    ):
        copy = pltpu.make_async_copy(src, dst, lsem.at[i])
        copy.start()
        loads.append(copy)

    owner = [own[b] for b in range(NB)]
    position = []
    for b in range(NB):
        before = jnp.int32(0)
        for b2 in range(b):
            before = before + (owner[b2] == owner[b]).astype(jnp.int32)
        position.append(before)

    lane = lax.broadcasted_iota(jnp.int32, (C, 128), 1)
    row = lax.broadcasted_iota(jnp.int32, (C, 128), 0)
    repeat = jnp.where(lax.rem(lane, C) == row, 1.0, 0.0).astype(BF16)
    wide[...] = dot_nn(grad[...].reshape(NB * R, C), repeat)
    group32 = lax.broadcasted_iota(jnp.int32, (R, 128), 1) // 32
    group16 = lax.broadcasted_iota(jnp.int32, (R, 128), 1) // 16
    zero = jnp.zeros((R, 128), F32)

    u = lax.rem(t, 4)
    place = [lax.rem(u + position[b], 4) for b in range(NB)]
    for o in range(NT):
        tile = zero
        for b in range(NB):
            chosen = jnp.where(owner[b] == o, place[b], -1)
            tile = jnp.where(group32 == chosen, wide[b * R : (b + 1) * R, :], tile)
        zsend[o] = tile.astype(BF16)

    pl.semaphore_wait(barrier, NT - 1 + ND - 1)

    zcopies = []
    for k in range(1, NT):
        o = lax.rem(t + k, NT)
        copy = pltpu.make_async_remote_copy(
            src_ref=zsend.at[o],
            dst_ref=zrecv.at[t],
            send_sem=zssem.at[k],
            recv_sem=zrsem.at[t],
            device_id={"tensor": o},
            device_id_type=MESH,
        )
        copy.start()
        zcopies.append(copy)
    zrecv[t] = zsend[t]

    wwide = dot_nn(weight[...].reshape(NB * R, C), repeat)
    for k in range(NB // 4):
        tile = zero
        for j in range(4):
            b = 4 * k + j
            tile = jnp.where(group32 == j, wwide[b * R : (b + 1) * R, :], tile)
        wrow[:, 128 * k : 128 * (k + 1)] = tile
    tall[...] = jnp.zeros((128, N), F32)
    for s in range(NS):
        dpad[s] = jnp.zeros((128, N), BF16)
        vpad[s] = jnp.zeros((128, N), BF16)

    for k in range(1, NT):
        o = lax.rem(t + k, NT)
        pltpu.make_async_remote_copy(
            src_ref=zsend.at[o],
            dst_ref=zrecv.at[o],
            send_sem=zssem.at[k],
            recv_sem=zrsem.at[o],
            device_id={"tensor": o},
            device_id_type=MESH,
        ).wait_recv()

    for k in range(4):
        tiles = [zrecv[4 * k + j].astype(F32) for j in range(4)]
        for s in range(NS):
            tile = zero
            for j in range(4):
                tile = jnp.where(group32 == (j + s) % 4, tiles[j], tile)
            if s:
                tile = pltpu.roll(tile, 128 - 32 * s, 1)
            gbuf[d, s, :, 128 * k : 128 * (k + 1)] = tile.astype(BF16)

    gather = PlaneGather(gbuf, gssem, grsem, x, y)
    m = lax.rem(d, 8)
    h = lax.rem(d, 2)

    def lane_groups(src, offset):
        parts = []
        for k in range(4):
            tile = zero
            for j in range(8):
                tile = jnp.where(group16 == (j + offset) % 8, src[8 * k + j].astype(F32), tile)
            if offset:
                tile = pltpu.roll(tile, 128 - 16 * offset, 1)
            parts.append(tile)
        return jnp.concatenate(parts, axis=1)

    def group_at(offset):
        return pl.ds(pl.multiple_of(16 * lax.rem(m + offset, 8), 16), 16)

    loads[1].wait()
    for s in range(NS):
        tall[group_at(s), :] = dot_nn(gbuf[d, s], qr[s])
    hsend[...] = tall[...].T.astype(BF16).reshape(ND, R, 128)
    hcopies = exchange(hsend, hrecv, hssem, hrsem)
    gather.along_y()

    loads[0].wait()
    received(hsend, hrecv, hssem, hrsem)
    for s in range(NS):
        half = lane_groups(hrecv, s).astype(BF16)
        turned = dot_nn(half, ql[s])
        high = turned.astype(BF16).astype(F32)
        tall[group_at(s), :] = high
        tall[group_at(s + 3), :] = turned - high
    rsend[...] = tall[...].T.astype(BF16).reshape(ND, R, 128)
    rcopies = exchange(rsend, rrecv, rssem, rrsem)
    for i in range(4):
        gather.along_x(i)

    for i in range(2, 4):
        loads[i].wait()
    received(rsend, rrecv, rssem, rrsem)
    stores = []
    for s in range(NS):
        rotated = lane_groups(rrecv, s) + lane_groups(rrecv, s + 3)
        first = beta_one * m1[s] + (1.0 - beta_one) * rotated
        second = beta_two * m2[s] + (1.0 - beta_two) * rotated * rotated
        m1[s] = first
        m2[s] = second
        direction = (first / (jnp.sqrt(second) + epsilon)).astype(BF16)
        dpad[s, group_at(s), :] = direction
    for i, (src, dst) in enumerate(((m1, nm1_hbm), (m2, nm2_hbm))):
        copy = pltpu.make_async_copy(src, dst, osem.at[i])
        copy.start()
        stores.append(copy)

    turned = dot_nt(qr[0], dpad[0])
    for s in range(1, NS):
        turned = turned + dot_nt(qr[s], dpad[s])
    bsend[...] = turned.astype(BF16).reshape(ND, R, 128)

    bcopies = exchange(bsend, brecv, bssem, brsem)

    for i in range(4, 8):
        gather.along_x(i)

    received(bsend, brecv, bssem, brsem)

    for s in range(NS):
        at = pl.multiple_of(32 * s + 16 * h, 16)
        vpad[s, pl.ds(at, 16), :] = lane_groups(brecv, s).astype(BF16)
    update = dot_nt(ql[0], vpad[0])
    for s in range(1, NS):
        update = update + dot_nt(ql[s], vpad[s])
    usend[...] = update.astype(BF16).reshape(ND, R, 128)
    ucopies = exchange(usend, urecv, ussem, ursem)

    for i in range(8):
        gather.onward(i)

    received(usend, urecv, ussem, ursem)

    for o in range(NT):
        ysend[o] = (urecv[2 * o].astype(F32) + urecv[2 * o + 1].astype(F32)).astype(BF16)
    ycopies = []
    for k in range(1, NT):
        o = lax.rem(t + k, NT)
        copy = pltpu.make_async_remote_copy(
            src_ref=ysend.at[o],
            dst_ref=yrecv.at[t],
            send_sem=yssem.at[k],
            recv_sem=yrsem.at[t],
            device_id={"tensor": o},
            device_id_type=MESH,
        )
        copy.start()
        ycopies.append(copy)
    yrecv[t] = ysend[t]
    for k in range(1, NT):
        o = lax.rem(t + k, NT)
        pltpu.make_async_remote_copy(
            src_ref=ysend.at[o],
            dst_ref=yrecv.at[o],
            send_sem=yssem.at[k],
            recv_sem=yrsem.at[o],
            device_id={"tensor": o},
            device_id_type=MESH,
        ).wait_recv()

    for k in range(NB // 4):
        tile = zero
        for j in range(4):
            b = 4 * k + j
            moved = pltpu.roll(
                yrecv[owner[b]].astype(F32), lax.rem(j - position[b] + 4, 4) * 32, 1
            )
            tile = jnp.where(group32 == j, moved, tile)
        old = wrow[:, 128 * k : 128 * (k + 1)]
        new = old - learn_rate * (tile + decay_rate * old)
        wbuf[d, :, 128 * k : 128 * (k + 1)] = new.astype(BF16)

    eye = jnp.where(
        lax.broadcasted_iota(jnp.int32, (128, 128), 0)
        == lax.broadcasted_iota(jnp.int32, (128, 128), 1),
        1.0,
        0.0,
    ).astype(BF16)
    final = PlaneGather(wbuf, wssem, wrsem, x, y)
    final.along_x(0)
    final.along_y()

    def whole(s):
        return gbuf[:, s].reshape(N, N)

    gather.last()
    gram_scale = 1.0 - beta_gram
    loads[4].wait()
    for s in range(NS):
        product = dot_nt(gbuf[d, s], whole(s))
        lg[s] = beta_gram * lg[s] + gram_scale * product
    copy = pltpu.make_async_copy(lg, nl_hbm, osem.at[2])
    copy.start()
    stores.append(copy)

    for i in range(1, 8):
        final.along_x(i)
        if i > 1:
            final.onward(i - 2)
    final.onward(6)
    final.onward(7)

    pick = jnp.where(
        lax.broadcasted_iota(jnp.int32, (R, 128), 1)
        == lax.broadcasted_iota(jnp.int32, (R, 128), 0) + 16 * m,
        1.0,
        0.0,
    ).astype(BF16)
    tile_start = pl.multiple_of(128 * (d // 8), 128)
    loads[5].wait()
    for s in range(NS):
        part = gbuf[:, s, :, pl.ds(tile_start, 128)].reshape(N, 128)
        columns = dot_nt(pick, part).astype(BF16)
        product = dot_nn(columns, whole(s))
        rg[s] = beta_gram * rg[s] + gram_scale * product
    copy = pltpu.make_async_copy(rg, nr_hbm, osem.at[3])
    copy.start()
    stores.append(copy)

    for dx in (0, 1, 3, 2):
        group = lax.rem(x + dx, NX)
        if dx == 2:
            final.last()
        rows = pl.ds(pl.multiple_of(NY * group, NY), NY)
        columns = pl.ds(pl.multiple_of(128 * group, 128), 128)
        for k in range(NB // 4):
            part = wbuf[rows, :, 128 * k : 128 * (k + 1)].reshape(128, 128)
            out_w[128 * k : 128 * (k + 1), columns] = dot_nt(eye, part).astype(BF16)
        copy = pltpu.make_async_copy(out_w.at[:, columns], w_hbm.at[:, columns], osem.at[4 + dx])
        copy.start()
        stores.append(copy)

    for copy in zcopies + hcopies + rcopies + bcopies + ucopies + ycopies:
        copy.wait_send()
    for copy in gather.started + final.started:
        copy.wait_send()
    for copy in stores:
        copy.wait()


def hand_over(
    w, nl, nr, nm1, nm2, w_out, nl_out, nr_out, nm1_out, nm2_out, w_v, nl_v, nr_v, nm1_v, nm2_v, sem
):
    triples = []
    for k in range(4):
        part = pl.ds(NB * C // 4 * k, NB * C // 4)
        triples.append((w.at[part], w_v.at[part], w_out.at[part]))
    triples += [(nl, nl_v, nl_out), (nr, nr_v, nr_out), (nm1, nm1_v, nm1_out), (nm2, nm2_v, nm2_out)]
    reads = [pltpu.make_async_copy(a, b, sem.at[0, i]) for i, (a, b, _) in enumerate(triples)]
    writes = [pltpu.make_async_copy(b, c, sem.at[1, i]) for i, (_, b, c) in enumerate(triples)]
    for copy in reads:
        copy.start()
    for read, write in zip(reads, writes):
        read.wait()
        write.start()
    for copy in writes:
        copy.wait()


def per_device(gradient, weight, owner_map, ql, qr, lg, rg, m1, m2):
    vmem = pl.BlockSpec(memory_space=pltpu.VMEM)
    anywhere = pl.BlockSpec(memory_space=pl.ANY)
    rows = jax.ShapeDtypeStruct((NS, R, N), F32)
    dma = pltpu.SemaphoreType.DMA
    outs = pl.pallas_call(
        kernel,
        out_shape=(jax.ShapeDtypeStruct((NB * C, N), BF16), rows, rows, rows, rows),
        in_specs=[pl.BlockSpec(memory_space=pltpu.SMEM), vmem, vmem] + [anywhere] * 6,
        out_specs=(anywhere,) * 5,
        scratch_shapes=[
            pltpu.VMEM((NB * C, N), BF16),
            pltpu.VMEM((NS, N, N), BF16),
            pltpu.VMEM((NS, N, N), BF16),
            pltpu.VMEM((NS, R, N), F32),
            pltpu.VMEM((NS, R, N), F32),
            pltpu.VMEM((NS, R, N), F32),
            pltpu.VMEM((NS, R, N), F32),
            pltpu.VMEM((NB * R, 128), F32),
            pltpu.VMEM((R, NB * C), F32),
            pltpu.VMEM((NT, R, 128), BF16),
            pltpu.VMEM((NT, R, 128), BF16),
            pltpu.VMEM((ND, NS, R, N), BF16),
            pltpu.VMEM((128, N), F32),
            pltpu.VMEM((ND, R, 128), BF16),
            pltpu.VMEM((ND, R, 128), BF16),
            pltpu.VMEM((ND, R, 128), BF16),
            pltpu.VMEM((ND, R, 128), BF16),
            pltpu.VMEM((NS, 128, N), BF16),
            pltpu.VMEM((ND, R, 128), BF16),
            pltpu.VMEM((ND, R, 128), BF16),
            pltpu.VMEM((NS, 128, N), BF16),
            pltpu.VMEM((ND, R, 128), BF16),
            pltpu.VMEM((ND, R, 128), BF16),
            pltpu.VMEM((NT, R, 128), BF16),
            pltpu.VMEM((NT, R, 128), BF16),
            pltpu.VMEM((ND, R, NB * C), BF16),
            dma((6,)),
            dma((8,)),
            dma((NT,)),
            dma((NT,)),
            dma((31,)),
            dma((ND,)),
            dma((ND,)),
            dma((ND,)),
            dma((ND,)),
            dma((ND,)),
            dma((ND,)),
            dma((ND,)),
            dma((ND,)),
            dma((ND,)),
            dma((NT,)),
            dma((NT,)),
            dma((31,)),
            dma((ND,)),
        ],
        compiler_params=pltpu.CompilerParams(
            collective_id=0, has_side_effects=True, vmem_limit_bytes=VMEM_LIMIT
        ),
        name="soap_step",
    )(owner_map.reshape(NB), gradient, weight, ql, qr, lg, rg, m1, m2)
    outs = pl.pallas_call(
        hand_over,
        out_shape=(jax.ShapeDtypeStruct((NB * C, N), BF16), rows, rows, rows, rows),
        in_specs=[anywhere] * 5,
        out_specs=(anywhere,) * 5,
        scratch_shapes=[pltpu.VMEM((NB * C, N), BF16)]
        + [pltpu.VMEM((NS, R, N), F32)] * 4
        + [dma((2, 8))],
        compiler_params=pltpu.CompilerParams(vmem_limit_bytes=VMEM_LIMIT),
        name="hand_over",
    )(*outs)
    new_weight = jnp.transpose(outs[0].reshape(NB, C, N), (0, 2, 1))
    return (new_weight,) + tuple(outs[1:])


def solution(mesh):
    in_specs = (
        P(None, "dp", "tensor"),
        P(None, "dp", "tensor"),
        P(),
        P("tensor", None, None),
        P("tensor", None, None),
        P("tensor", "dp", None),
        P("tensor", "dp", None),
        P("tensor", "dp", None),
        P("tensor", "dp", None),
    )
    out_specs = (
        P(None, None, "tensor"),
        P("tensor", "dp", None),
        P("tensor", "dp", None),
        P("tensor", "dp", None),
        P("tensor", "dp", None),
    )
    return jax.shard_map(
        per_device, mesh=mesh, in_specs=in_specs, out_specs=out_specs, check_vma=False
    )
```

```python
import jax
import jax.numpy as jnp
from jax import lax
from jax.experimental import pallas as pl
from jax.experimental.pallas import tpu as pltpu
from jax.sharding import PartitionSpec as P

beta_one = 0.9
beta_two = 0.999
beta_gram = 0.95
epsilon = 1e-08
learn_rate = 0.01
decay_rate = 0.1

MESH = pl.DeviceIdType.MESH
F32 = jnp.float32
BF16 = jnp.bfloat16

NX = 4
NY = 8
ND = NX * NY
NT = 16
NB = 24
NS = 3
N = 512
R = 16
C = 32
VMEM_LIMIT = 56 * 1024 * 1024


def dot_nt(a, b):
    return lax.dot_general(a, b, (((1,), (1,)), ((), ())), preferred_element_type=F32)


def dot_nn(a, b):
    return lax.dot_general(a, b, (((1,), (0,)), ((), ())), preferred_element_type=F32)


class PlaneGather:
    legs = (1, -1, 2, -2, 3, -3, 4)

    def __init__(self, buf, ssem, rsem, x, y):
        self.buf, self.ssem, self.rsem, self.x, self.y = buf, ssem, rsem, x, y
        self.started = []

    def place(self, dx, dy):
        return lax.rem(self.x + dx + NX, NX) * NY + lax.rem(self.y + dy + NY, NY)

    def copy_of(self, dx, dy, tx, ty):
        src = self.place(dx, dy)
        return pltpu.make_async_remote_copy(
            src_ref=self.buf.at[src],
            dst_ref=self.buf.at[src],
            send_sem=self.ssem.at[len(self.started)],
            recv_sem=self.rsem.at[src],
            device_id={"dp": self.place(tx, ty)},
            device_id_type=MESH,
        )

    def send(self, dx, dy, tx, ty):
        copy = self.copy_of(dx, dy, tx, ty)
        copy.start()
        self.started.append(copy)

    def arrive(self, dx, dy):
        src = self.place(dx, dy)
        pltpu.make_async_remote_copy(
            src_ref=self.buf.at[src],
            dst_ref=self.buf.at[src],
            send_sem=self.ssem.at[0],
            recv_sem=self.rsem.at[src],
            device_id={"dp": self.place(1, 0)},
            device_id_type=MESH,
        ).wait_recv()

    def along_y(self):
        for dy in self.legs:
            self.send(0, 0, 0, dy)

    def along_x(self, i):
        dy = 0
        if i > 0:
            dy = -self.legs[i - 1]
            self.arrive(0, dy)
        self.send(0, dy, 1, 0)
        self.send(0, dy, -1, 0)

    def onward(self, i):
        dy = 0 if i == 0 else -self.legs[i - 1]
        self.arrive(-1, dy)
        self.arrive(1, dy)
        if i % 2 == 0:
            self.send(-1, dy, 1, 0)
        else:
            self.send(1, dy, -1, 0)

    def last(self):
        for dy in (0,) + tuple(-k for k in self.legs):
            self.arrive(2, dy)


def kernel(
    own,
    grad,
    weight,
    ql_hbm,
    qr_hbm,
    lg_hbm,
    rg_hbm,
    m1_hbm,
    m2_hbm,
    w_hbm,
    nl_hbm,
    nr_hbm,
    nm1_hbm,
    nm2_hbm,
    out_w,
    ql,
    qr,
    lg,
    rg,
    m1,
    m2,
    wide,
    wrow,
    zsend,
    zrecv,
    gbuf,
    tall,
    hsend,
    hrecv,
    rsend,
    rrecv,
    dpad,
    bsend,
    brecv,
    vpad,
    usend,
    urecv,
    wbuf,
    lsem,
    osem,
    zssem,
    zrsem,
    gssem,
    grsem,
    hssem,
    hrsem,
    rssem,
    rrsem,
    bssem,
    brsem,
    ussem,
    ursem,
    wssem,
    wrsem,
):
    d = lax.axis_index("dp")
    t = lax.axis_index("tensor")
    x = d // NY
    y = lax.rem(d, NY)

    barrier = pltpu.get_barrier_semaphore()
    for k in range(1, NT):
        pl.semaphore_signal(
            barrier, inc=1, device_id={"tensor": lax.rem(t + k, NT)}, device_id_type=MESH
        )
    for k in range(1, ND):
        pl.semaphore_signal(
            barrier, inc=1, device_id={"dp": lax.rem(d + k, ND)}, device_id_type=MESH
        )

    def exchange(src, dst, ssem, rsem):
        copies = []
        for dx in (2, 1, 3, 0):
            for dy in (4, 3, 5, 2, 6, 1, 7, 0):
                if dx == 0 and dy == 0:
                    continue
                k = dx * NY + dy
                to = lax.rem(x + dx, NX) * NY + lax.rem(y + dy, NY)
                copy = pltpu.make_async_remote_copy(
                    src_ref=src.at[to],
                    dst_ref=dst.at[d],
                    send_sem=ssem.at[k],
                    recv_sem=rsem.at[d],
                    device_id={"dp": to},
                    device_id_type=MESH,
                )
                copy.start()
                copies.append(copy)
        dst[d] = src[d]
        return copies

    def received(src, dst, ssem, rsem):
        for k in range(1, ND):
            o = lax.rem(d + k, ND)
            pltpu.make_async_remote_copy(
                src_ref=src.at[o],
                dst_ref=dst.at[o],
                send_sem=ssem.at[k],
                recv_sem=rsem.at[o],
                device_id={"dp": o},
                device_id_type=MESH,
            ).wait_recv()

    target = d // 2
    slot = 2 * t + lax.rem(d, 2)
    apart = target != t
    for i in range(ND):
        at = 2 * t + i % 2

        @pl.when(jnp.logical_or(apart, i != slot))
        def _():
            pl.semaphore_signal(
                barrier, inc=1, device_id={"dp": at, "tensor": i // 2}, device_id_type=MESH
            )

    loads = []
    for i, (src, dst) in enumerate(
        ((ql_hbm, ql), (qr_hbm, qr), (m1_hbm, m1), (m2_hbm, m2), (lg_hbm, lg), (rg_hbm, rg))
    ):
        copy = pltpu.make_async_copy(src, dst, lsem.at[i])
        copy.start()
        loads.append(copy)

    owner = [own[b] for b in range(NB)]
    position = []
    for b in range(NB):
        before = jnp.int32(0)
        for b2 in range(b):
            before = before + (owner[b2] == owner[b]).astype(jnp.int32)
        position.append(before)

    lane = lax.broadcasted_iota(jnp.int32, (C, 128), 1)
    row = lax.broadcasted_iota(jnp.int32, (C, 128), 0)
    repeat = jnp.where(lax.rem(lane, C) == row, 1.0, 0.0).astype(BF16)
    wide[...] = dot_nn(grad[...].reshape(NB * R, C), repeat)
    group32 = lax.broadcasted_iota(jnp.int32, (R, 128), 1) // 32
    group16 = lax.broadcasted_iota(jnp.int32, (R, 128), 1) // 16
    zero = jnp.zeros((R, 128), F32)

    u = lax.rem(t, 4)
    place = [lax.rem(u + position[b], 4) for b in range(NB)]
    for o in range(NT):
        tile = zero
        for b in range(NB):
            chosen = jnp.where(owner[b] == o, place[b], -1)
            tile = jnp.where(group32 == chosen, wide[b * R : (b + 1) * R, :], tile)
        zsend[o] = tile.astype(BF16)

    pl.semaphore_wait(barrier, NT - 1 + ND - 1 + ND - 1 + apart.astype(jnp.int32))

    zcopies = []
    for k in range(1, NT):
        o = lax.rem(t + k, NT)
        copy = pltpu.make_async_remote_copy(
            src_ref=zsend.at[o],
            dst_ref=zrecv.at[t],
            send_sem=zssem.at[k],
            recv_sem=zrsem.at[t],
            device_id={"tensor": o},
            device_id_type=MESH,
        )
        copy.start()
        zcopies.append(copy)
    zrecv[t] = zsend[t]

    wwide = dot_nn(weight[...].reshape(NB * R, C), repeat)
    for k in range(NB // 4):
        tile = zero
        for j in range(4):
            b = 4 * k + j
            tile = jnp.where(group32 == j, wwide[b * R : (b + 1) * R, :], tile)
        wrow[:, 128 * k : 128 * (k + 1)] = tile
    tall[...] = jnp.zeros((128, N), F32)
    for s in range(NS):
        dpad[s] = jnp.zeros((128, N), BF16)
        vpad[s] = jnp.zeros((128, N), BF16)

    for k in range(1, NT):
        o = lax.rem(t + k, NT)
        pltpu.make_async_remote_copy(
            src_ref=zsend.at[o],
            dst_ref=zrecv.at[o],
            send_sem=zssem.at[k],
            recv_sem=zrsem.at[o],
            device_id={"tensor": o},
            device_id_type=MESH,
        ).wait_recv()

    for k in range(4):
        tiles = [zrecv[4 * k + j].astype(F32) for j in range(4)]
        for s in range(NS):
            tile = zero
            for j in range(4):
                tile = jnp.where(group32 == (j + s) % 4, tiles[j], tile)
            if s:
                tile = pltpu.roll(tile, 128 - 32 * s, 1)
            gbuf[d, s, :, 128 * k : 128 * (k + 1)] = tile.astype(BF16)

    gather = PlaneGather(gbuf, gssem, grsem, x, y)
    m = lax.rem(d, 8)
    h = lax.rem(d, 2)

    def lane_groups(src, offset):
        parts = []
        for k in range(4):
            tile = zero
            for j in range(8):
                tile = jnp.where(group16 == (j + offset) % 8, src[8 * k + j].astype(F32), tile)
            if offset:
                tile = pltpu.roll(tile, 128 - 16 * offset, 1)
            parts.append(tile)
        return jnp.concatenate(parts, axis=1)

    def group_at(offset):
        return pl.ds(pl.multiple_of(16 * lax.rem(m + offset, 8), 16), 16)

    loads[1].wait()
    for s in range(NS):
        tall[group_at(s), :] = dot_nn(gbuf[d, s], qr[s])
    hsend[...] = tall[...].T.astype(BF16).reshape(ND, R, 128)
    hcopies = exchange(hsend, hrecv, hssem, hrsem)
    gather.along_y()
    gather.along_x(0)

    loads[0].wait()
    received(hsend, hrecv, hssem, hrsem)
    for s in range(NS):
        half = lane_groups(hrecv, s).astype(BF16)
        turned = dot_nn(half, ql[s])
        high = turned.astype(BF16).astype(F32)
        tall[group_at(s), :] = high
        tall[group_at(s + 3), :] = turned - high
    rsend[...] = tall[...].T.astype(BF16).reshape(ND, R, 128)
    rcopies = exchange(rsend, rrecv, rssem, rrsem)
    for i in range(1, 5):
        gather.along_x(i)

    for i in range(2, 4):
        loads[i].wait()
    received(rsend, rrecv, rssem, rrsem)
    stores = []
    for s in range(NS):
        rotated = lane_groups(rrecv, s) + lane_groups(rrecv, s + 3)
        first = beta_one * m1[s] + (1.0 - beta_one) * rotated
        second = beta_two * m2[s] + (1.0 - beta_two) * rotated * rotated
        m1[s] = first
        m2[s] = second
        direction = (first / (jnp.sqrt(second) + epsilon)).astype(BF16)
        dpad[s, group_at(s), :] = direction
    for i, (src, dst) in enumerate(((m1, nm1_hbm), (m2, nm2_hbm))):
        copy = pltpu.make_async_copy(src, dst, osem.at[i])
        copy.start()
        stores.append(copy)

    turned = dot_nt(qr[0], dpad[0])
    for s in range(1, NS):
        turned = turned + dot_nt(qr[s], dpad[s])
    bsend[...] = turned.astype(BF16).reshape(ND, R, 128)

    bcopies = exchange(bsend, brecv, bssem, brsem)

    for i in range(5, 8):
        gather.along_x(i)
    for i in range(8):
        gather.onward(i)

    received(bsend, brecv, bssem, brsem)

    for s in range(NS):
        at = pl.multiple_of(32 * s + 16 * h, 16)
        vpad[s, pl.ds(at, 16), :] = lane_groups(brecv, s).astype(BF16)
    update = dot_nt(ql[0], vpad[0])
    for s in range(1, NS):
        update = update + dot_nt(ql[s], vpad[s])
    usend[...] = update.astype(BF16).reshape(ND, R, 128)

    def update_copy(dx, dy):
        to = lax.rem(x + dx, NX) * NY + lax.rem(y + dy, NY)
        return pltpu.make_async_remote_copy(
            src_ref=usend.at[to],
            dst_ref=urecv.at[slot],
            send_sem=ussem.at[dx * NY + dy],
            recv_sem=ursem.at[slot],
            device_id={"dp": to, "tensor": target},
            device_id_type=MESH,
        )

    ucopies = []
    for dx in (2, 1, 3, 0):
        for dy in (4, 3, 5, 2, 6, 1, 7, 0):
            if dx or dy:
                copy = update_copy(dx, dy)
                copy.start()
                ucopies.append(copy)

    @pl.when(apart)
    def _():
        update_copy(0, 0).start()

    @pl.when(jnp.logical_not(apart))
    def _():
        urecv[slot] = usend[d]

    def whole(s):
        return gbuf[:, s].reshape(N, N)

    gather.last()
    gram_scale = 1.0 - beta_gram
    loads[4].wait()
    for s in range(NS):
        product = dot_nt(gbuf[d, s], whole(s))
        lg[s] = beta_gram * lg[s] + gram_scale * product
    copy = pltpu.make_async_copy(lg, nl_hbm, osem.at[2])
    copy.start()
    stores.append(copy)

    for i in range(ND):

        @pl.when(jnp.logical_or(apart, i != slot))
        def _():
            pltpu.make_async_remote_copy(
                src_ref=usend.at[0],
                dst_ref=urecv.at[i],
                send_sem=ussem.at[0],
                recv_sem=ursem.at[i],
                device_id={"dp": 2 * t + i % 2, "tensor": i // 2},
                device_id_type=MESH,
            ).wait_recv()

    for k in range(NB // 4):
        tile = zero
        for j in range(4):
            b = 4 * k + j
            pair = urecv[2 * owner[b]].astype(F32) + urecv[2 * owner[b] + 1].astype(F32)
            moved = pltpu.roll(pair, lax.rem(j - position[b] + 4, 4) * 32, 1)
            tile = jnp.where(group32 == j, moved, tile)
        old = wrow[:, 128 * k : 128 * (k + 1)]
        new = old - learn_rate * (tile + decay_rate * old)
        wbuf[d, :, 128 * k : 128 * (k + 1)] = new.astype(BF16)

    eye = jnp.where(
        lax.broadcasted_iota(jnp.int32, (128, 128), 0)
        == lax.broadcasted_iota(jnp.int32, (128, 128), 1),
        1.0,
        0.0,
    ).astype(BF16)
    final = PlaneGather(wbuf, wssem, wrsem, x, y)
    final.along_x(0)
    final.along_y()

    for i in range(1, 8):
        final.along_x(i)
        if i > 1:
            final.onward(i - 2)
    final.onward(6)
    final.onward(7)

    pick = jnp.where(
        lax.broadcasted_iota(jnp.int32, (R, 128), 1)
        == lax.broadcasted_iota(jnp.int32, (R, 128), 0) + 16 * m,
        1.0,
        0.0,
    ).astype(BF16)
    tile_start = pl.multiple_of(128 * (d // 8), 128)
    loads[5].wait()
    for s in range(NS):
        part = gbuf[:, s, :, pl.ds(tile_start, 128)].reshape(N, 128)
        columns = dot_nt(pick, part).astype(BF16)
        product = dot_nn(columns, whole(s))
        rg[s] = beta_gram * rg[s] + gram_scale * product
    copy = pltpu.make_async_copy(rg, nr_hbm, osem.at[3])
    copy.start()
    stores.append(copy)

    for dx in (0, 1, 3, 2):
        group = lax.rem(x + dx, NX)
        if dx == 2:
            final.last()
        rows = pl.ds(pl.multiple_of(NY * group, NY), NY)
        columns = pl.ds(pl.multiple_of(128 * group, 128), 128)
        for k in range(NB // 4):
            part = wbuf[rows, :, 128 * k : 128 * (k + 1)].reshape(128, 128)
            out_w[128 * k : 128 * (k + 1), columns] = dot_nt(eye, part).astype(BF16)
        copy = pltpu.make_async_copy(out_w.at[:, columns], w_hbm.at[:, columns], osem.at[4 + dx])
        copy.start()
        stores.append(copy)

    for copy in zcopies + hcopies + rcopies + bcopies + ucopies:
        copy.wait_send()
    for copy in gather.started + final.started:
        copy.wait_send()

    @pl.when(apart)
    def _():
        update_copy(0, 0).wait_send()

    for copy in stores:
        copy.wait()


def hand_over(
    w, nl, nr, nm1, nm2, w_out, nl_out, nr_out, nm1_out, nm2_out, w_v, nl_v, nr_v, nm1_v, nm2_v, sem
):
    triples = []
    for k in range(4):
        part = pl.ds(NB * C // 4 * k, NB * C // 4)
        triples.append((w.at[part], w_v.at[part], w_out.at[part]))
    triples += [(nl, nl_v, nl_out), (nr, nr_v, nr_out), (nm1, nm1_v, nm1_out), (nm2, nm2_v, nm2_out)]
    reads = [pltpu.make_async_copy(a, b, sem.at[0, i]) for i, (a, b, _) in enumerate(triples)]
    writes = [pltpu.make_async_copy(b, c, sem.at[1, i]) for i, (_, b, c) in enumerate(triples)]
    for copy in reads:
        copy.start()
    for read, write in zip(reads, writes):
        read.wait()
        write.start()
    for copy in writes:
        copy.wait()


def per_device(gradient, weight, owner_map, ql, qr, lg, rg, m1, m2):
    vmem = pl.BlockSpec(memory_space=pltpu.VMEM)
    anywhere = pl.BlockSpec(memory_space=pl.ANY)
    rows = jax.ShapeDtypeStruct((NS, R, N), F32)
    dma = pltpu.SemaphoreType.DMA
    outs = pl.pallas_call(
        kernel,
        out_shape=(jax.ShapeDtypeStruct((NB * C, N), BF16), rows, rows, rows, rows),
        in_specs=[pl.BlockSpec(memory_space=pltpu.SMEM), vmem, vmem] + [anywhere] * 6,
        out_specs=(anywhere,) * 5,
        scratch_shapes=[
            pltpu.VMEM((NB * C, N), BF16),
            pltpu.VMEM((NS, N, N), BF16),
            pltpu.VMEM((NS, N, N), BF16),
            pltpu.VMEM((NS, R, N), F32),
            pltpu.VMEM((NS, R, N), F32),
            pltpu.VMEM((NS, R, N), F32),
            pltpu.VMEM((NS, R, N), F32),
            pltpu.VMEM((NB * R, 128), F32),
            pltpu.VMEM((R, NB * C), F32),
            pltpu.VMEM((NT, R, 128), BF16),
            pltpu.VMEM((NT, R, 128), BF16),
            pltpu.VMEM((ND, NS, R, N), BF16),
            pltpu.VMEM((128, N), F32),
            pltpu.VMEM((ND, R, 128), BF16),
            pltpu.VMEM((ND, R, 128), BF16),
            pltpu.VMEM((ND, R, 128), BF16),
            pltpu.VMEM((ND, R, 128), BF16),
            pltpu.VMEM((NS, 128, N), BF16),
            pltpu.VMEM((ND, R, 128), BF16),
            pltpu.VMEM((ND, R, 128), BF16),
            pltpu.VMEM((NS, 128, N), BF16),
            pltpu.VMEM((ND, R, 128), BF16),
            pltpu.VMEM((ND, R, 128), BF16),
            pltpu.VMEM((ND, R, NB * C), BF16),
            dma((6,)),
            dma((8,)),
            dma((NT,)),
            dma((NT,)),
            dma((31,)),
            dma((ND,)),
            dma((ND,)),
            dma((ND,)),
            dma((ND,)),
            dma((ND,)),
            dma((ND,)),
            dma((ND,)),
            dma((ND,)),
            dma((ND,)),
            dma((31,)),
            dma((ND,)),
        ],
        compiler_params=pltpu.CompilerParams(
            collective_id=0, has_side_effects=True, vmem_limit_bytes=VMEM_LIMIT
        ),
        name="soap_step",
    )(owner_map.reshape(NB), gradient, weight, ql, qr, lg, rg, m1, m2)
    outs = pl.pallas_call(
        hand_over,
        out_shape=(jax.ShapeDtypeStruct((NB * C, N), BF16), rows, rows, rows, rows),
        in_specs=[anywhere] * 5,
        out_specs=(anywhere,) * 5,
        scratch_shapes=[pltpu.VMEM((NB * C, N), BF16)]
        + [pltpu.VMEM((NS, R, N), F32)] * 4
        + [dma((2, 8))],
        compiler_params=pltpu.CompilerParams(vmem_limit_bytes=VMEM_LIMIT),
        name="hand_over",
    )(*outs)
    new_weight = jnp.transpose(outs[0].reshape(NB, C, N), (0, 2, 1))
    return (new_weight,) + tuple(outs[1:])


def solution(mesh):
    in_specs = (
        P(None, "dp", "tensor"),
        P(None, "dp", "tensor"),
        P(),
        P("tensor", None, None),
        P("tensor", None, None),
        P("tensor", "dp", None),
        P("tensor", "dp", None),
        P("tensor", "dp", None),
        P("tensor", "dp", None),
    )
    out_specs = (
        P(None, None, "tensor"),
        P("tensor", "dp", None),
        P("tensor", "dp", None),
        P("tensor", "dp", None),
        P("tensor", "dp", None),
    )
    return jax.shard_map(
        per_device, mesh=mesh, in_specs=in_specs, out_specs=out_specs, check_vma=False
    )
```

```python
import jax
import jax.numpy as jnp
from jax import lax
from jax.experimental import pallas as pl
from jax.experimental.pallas import tpu as pltpu
from jax.sharding import PartitionSpec as P

beta_one = 0.9
beta_two = 0.999
beta_gram = 0.95
epsilon = 1e-08
learn_rate = 0.01
decay_rate = 0.1

MESH = pl.DeviceIdType.MESH
F32 = jnp.float32
BF16 = jnp.bfloat16

NX = 4
NY = 8
ND = NX * NY
NT = 16
NB = 24
NS = 3
N = 512
R = 16
C = 32
VMEM_LIMIT = 56 * 1024 * 1024


def dot_nt(a, b):
    return lax.dot_general(a, b, (((1,), (1,)), ((), ())), preferred_element_type=F32)


def dot_nn(a, b):
    return lax.dot_general(a, b, (((1,), (0,)), ((), ())), preferred_element_type=F32)


class PlaneGather:
    legs = (1, -1, 2, -2, 3, -3, 4)

    def __init__(self, buf, ssem, rsem, x, y):
        self.buf, self.ssem, self.rsem, self.x, self.y = buf, ssem, rsem, x, y
        self.started = []

    def place(self, dx, dy):
        return lax.rem(self.x + dx + NX, NX) * NY + lax.rem(self.y + dy + NY, NY)

    def copy_of(self, dx, dy, tx, ty):
        src = self.place(dx, dy)
        return pltpu.make_async_remote_copy(
            src_ref=self.buf.at[src],
            dst_ref=self.buf.at[src],
            send_sem=self.ssem.at[0],
            recv_sem=self.rsem.at[src],
            device_id={"dp": self.place(tx, ty)},
            device_id_type=MESH,
        )

    def send(self, dx, dy, tx, ty):
        copy = self.copy_of(dx, dy, tx, ty)
        copy.start()
        self.started.append(copy)

    def arrive(self, dx, dy):
        src = self.place(dx, dy)
        pltpu.make_async_remote_copy(
            src_ref=self.buf.at[src],
            dst_ref=self.buf.at[src],
            send_sem=self.ssem.at[0],
            recv_sem=self.rsem.at[src],
            device_id={"dp": self.place(1, 0)},
            device_id_type=MESH,
        ).wait_recv()

    def along_y(self):
        for dy in self.legs:
            self.send(0, 0, 0, dy)

    def begin(self):
        for tx, ty in ((0, 1), (0, -1), (1, 0), (-1, 0)):
            self.send(0, 0, tx, ty)

    def ring(self, k):
        for dy, ty, end in ((-k, 1, 4), (k, -1, 3)):
            if k <= end:
                self.arrive(0, dy)
                if k < end:
                    self.send(0, dy, 0, ty)
                self.send(0, dy, 1, 0)
                self.send(0, dy, -1, 0)

    def along_x(self, i):
        dy = 0
        if i > 0:
            dy = -self.legs[i - 1]
            self.arrive(0, dy)
        self.send(0, dy, 1, 0)
        self.send(0, dy, -1, 0)

    def onward(self, i):
        dy = 0 if i == 0 else -self.legs[i - 1]
        self.arrive(-1, dy)
        self.arrive(1, dy)
        if i % 2 == 0:
            self.send(-1, dy, 1, 0)
        else:
            self.send(1, dy, -1, 0)

    def finish(self):
        chunks = self.buf.at[pl.ds(0, len(self.started))]
        pltpu.make_async_remote_copy(
            src_ref=chunks,
            dst_ref=chunks,
            send_sem=self.ssem.at[0],
            recv_sem=self.rsem.at[0],
            device_id={"dp": self.place(1, 0)},
            device_id_type=MESH,
        ).wait_send()

    def last(self):
        for dy in (0,) + tuple(-k for k in self.legs):
            self.arrive(2, dy)


def kernel(
    own,
    grad,
    weight,
    ql_hbm,
    qr_hbm,
    lg_hbm,
    rg_hbm,
    m1_hbm,
    m2_hbm,
    w_hbm,
    nl_hbm,
    nr_hbm,
    nm1_hbm,
    nm2_hbm,
    out_w,
    ql,
    qr,
    lg,
    rg,
    m1,
    m2,
    wide,
    wrow,
    zsend,
    zrecv,
    gbuf,
    tall,
    hsend,
    hrecv,
    rsend,
    rrecv,
    dpad,
    bsend,
    brecv,
    vpad,
    usend,
    urecv,
    ysend,
    yrecv,
    wbuf,
    lsem,
    osem,
    zssem,
    zrsem,
    gssem,
    grsem,
    hssem,
    hrsem,
    rssem,
    rrsem,
    bssem,
    brsem,
    ussem,
    ursem,
    yssem,
    yrsem,
    wssem,
    wrsem,
):
    d = lax.axis_index("dp")
    t = lax.axis_index("tensor")
    x = d // NY
    y = lax.rem(d, NY)

    barrier = pltpu.get_barrier_semaphore()
    for k in range(1, NT):
        pl.semaphore_signal(
            barrier, inc=1, device_id={"tensor": lax.rem(t + k, NT)}, device_id_type=MESH
        )
    for k in range(1, ND):
        pl.semaphore_signal(
            barrier, inc=1, device_id={"dp": lax.rem(d + k, ND)}, device_id_type=MESH
        )

    def exchange(src, dst, ssem, rsem):
        for dx in (2, 1, 3, 0):
            for dy in (4, 3, 5, 2, 6, 1, 7, 0):
                if dx == 0 and dy == 0:
                    continue
                to = lax.rem(x + dx, NX) * NY + lax.rem(y + dy, NY)
                copy = pltpu.make_async_remote_copy(
                    src_ref=src.at[to],
                    dst_ref=dst.at[d],
                    send_sem=ssem.at[0],
                    recv_sem=rsem.at[0],
                    device_id={"dp": to},
                    device_id_type=MESH,
                )
                copy.start()
        dst[d] = src[d]

    def all_of(axis, size, me, src, dst, ssem, rsem):
        return pltpu.make_async_remote_copy(
            src_ref=src.at[pl.ds(0, size - 1)],
            dst_ref=dst.at[pl.ds(0, size - 1)],
            send_sem=ssem.at[0],
            recv_sem=rsem.at[0],
            device_id={axis: lax.rem(me + 1, size)},
            device_id_type=MESH,
        )

    def received(src, dst, ssem, rsem):
        all_of("dp", ND, d, src, dst, ssem, rsem).wait_recv()

    loads = []
    for i, (src, dst) in enumerate(
        ((ql_hbm, ql), (qr_hbm, qr), (m1_hbm, m1), (m2_hbm, m2), (lg_hbm, lg), (rg_hbm, rg))
    ):
        copy = pltpu.make_async_copy(src, dst, lsem.at[i])
        copy.start()
        loads.append(copy)

    owner = [own[b] for b in range(NB)]
    position = []
    for b in range(NB):
        before = jnp.int32(0)
        for b2 in range(b):
            before = before + (owner[b2] == owner[b]).astype(jnp.int32)
        position.append(before)

    lane = lax.broadcasted_iota(jnp.int32, (C, 128), 1)
    row = lax.broadcasted_iota(jnp.int32, (C, 128), 0)
    repeat = jnp.where(lax.rem(lane, C) == row, 1.0, 0.0).astype(BF16)
    wide[...] = dot_nn(grad[...].reshape(NB * R, C), repeat)
    group32 = lax.broadcasted_iota(jnp.int32, (R, 128), 1) // 32
    group16 = lax.broadcasted_iota(jnp.int32, (R, 128), 1) // 16
    zero = jnp.zeros((R, 128), F32)

    u = lax.rem(t, 4)
    place = [lax.rem(u + position[b], 4) for b in range(NB)]
    for o in range(NT):
        tile = zero
        for b in range(NB):
            chosen = jnp.where(owner[b] == o, place[b], -1)
            tile = jnp.where(group32 == chosen, wide[b * R : (b + 1) * R, :], tile)
        zsend[o] = tile.astype(BF16)

    pl.semaphore_wait(barrier, NT - 1 + ND - 1)

    for k in range(1, NT):
        o = lax.rem(t + k, NT)
        copy = pltpu.make_async_remote_copy(
            src_ref=zsend.at[o],
            dst_ref=zrecv.at[t],
            send_sem=zssem.at[0],
            recv_sem=zrsem.at[0],
            device_id={"tensor": o},
            device_id_type=MESH,
        )
        copy.start()
    zrecv[t] = zsend[t]

    wwide = dot_nn(weight[...].reshape(NB * R, C), repeat)
    for k in range(NB // 4):
        tile = zero
        for j in range(4):
            b = 4 * k + j
            tile = jnp.where(group32 == j, wwide[b * R : (b + 1) * R, :], tile)
        wrow[:, 128 * k : 128 * (k + 1)] = tile
    tall[...] = jnp.zeros((128, N), F32)
    for s in range(NS):
        dpad[s] = jnp.zeros((128, N), BF16)
        vpad[s] = jnp.zeros((128, N), BF16)

    all_of("tensor", NT, t, zsend, zrecv, zssem, zrsem).wait_recv()

    for k in range(4):
        tiles = [zrecv[4 * k + j].astype(F32) for j in range(4)]
        for s in range(NS):
            tile = zero
            for j in range(4):
                tile = jnp.where(group32 == (j + s) % 4, tiles[j], tile)
            if s:
                tile = pltpu.roll(tile, 128 - 32 * s, 1)
            gbuf[d, s, :, 128 * k : 128 * (k + 1)] = tile.astype(BF16)

    gather = PlaneGather(gbuf, gssem, grsem, x, y)
    m = lax.rem(d, 8)
    h = lax.rem(d, 2)

    def lane_groups(src, offset):
        parts = []
        for k in range(4):
            tile = zero
            for j in range(8):
                tile = jnp.where(group16 == (j + offset) % 8, src[8 * k + j].astype(F32), tile)
            if offset:
                tile = pltpu.roll(tile, 128 - 16 * offset, 1)
            parts.append(tile)
        return jnp.concatenate(parts, axis=1)

    def group_at(offset):
        return pl.ds(pl.multiple_of(16 * lax.rem(m + offset, 8), 16), 16)

    loads[1].wait()
    for s in range(NS):
        tall[group_at(s), :] = dot_nn(gbuf[d, s], qr[s])
    hsend[...] = tall[...].T.astype(BF16).reshape(ND, R, 128)
    exchange(hsend, hrecv, hssem, hrsem)
    gather.begin()
    gather.ring(1)

    loads[0].wait()
    received(hsend, hrecv, hssem, hrsem)
    for s in range(NS):
        half = lane_groups(hrecv, s).astype(BF16)
        turned = dot_nn(half, ql[s])
        high = turned.astype(BF16).astype(F32)
        tall[group_at(s), :] = high
        tall[group_at(s + 3), :] = turned - high
    rsend[...] = tall[...].T.astype(BF16).reshape(ND, R, 128)
    exchange(rsend, rrecv, rssem, rrsem)
    gather.ring(2)
    gather.ring(3)

    for i in range(2, 4):
        loads[i].wait()
    received(rsend, rrecv, rssem, rrsem)
    stores = []
    for s in range(NS):
        rotated = lane_groups(rrecv, s) + lane_groups(rrecv, s + 3)
        first = beta_one * m1[s] + (1.0 - beta_one) * rotated
        second = beta_two * m2[s] + (1.0 - beta_two) * rotated * rotated
        m1[s] = first
        m2[s] = second
        direction = (first / (jnp.sqrt(second) + epsilon)).astype(BF16)
        dpad[s, group_at(s), :] = direction
    for i, (src, dst) in enumerate(((m1, nm1_hbm), (m2, nm2_hbm))):
        copy = pltpu.make_async_copy(src, dst, osem.at[i])
        copy.start()
        stores.append(copy)

    turned = dot_nt(qr[0], dpad[0])
    for s in range(1, NS):
        turned = turned + dot_nt(qr[s], dpad[s])
    bsend[...] = turned.astype(BF16).reshape(ND, R, 128)

    exchange(bsend, brecv, bssem, brsem)

    gather.ring(4)
    for i in range(4):
        gather.onward(i)

    received(bsend, brecv, bssem, brsem)

    for s in range(NS):
        at = pl.multiple_of(32 * s + 16 * h, 16)
        vpad[s, pl.ds(at, 16), :] = lane_groups(brecv, s).astype(BF16)
    update = dot_nt(ql[0], vpad[0])
    for s in range(1, NS):
        update = update + dot_nt(ql[s], vpad[s])
    usend[...] = update.astype(BF16).reshape(ND, R, 128)
    exchange(usend, urecv, ussem, ursem)

    for i in range(4, 8):
        gather.onward(i)

    received(usend, urecv, ussem, ursem)

    for o in range(NT):
        ysend[o] = (urecv[2 * o].astype(F32) + urecv[2 * o + 1].astype(F32)).astype(BF16)
    for k in range(1, NT):
        o = lax.rem(t + k, NT)
        copy = pltpu.make_async_remote_copy(
            src_ref=ysend.at[o],
            dst_ref=yrecv.at[t],
            send_sem=yssem.at[0],
            recv_sem=yrsem.at[0],
            device_id={"tensor": o},
            device_id_type=MESH,
        )
        copy.start()
    yrecv[t] = ysend[t]

    def whole(s):
        return gbuf[:, s].reshape(N, N)

    gather.last()
    gram_scale = 1.0 - beta_gram
    loads[4].wait()
    for s in range(NS):
        product = dot_nt(gbuf[d, s], whole(s))
        lg[s] = beta_gram * lg[s] + gram_scale * product
    copy = pltpu.make_async_copy(lg, nl_hbm, osem.at[2])
    copy.start()
    stores.append(copy)

    all_of("tensor", NT, t, ysend, yrecv, yssem, yrsem).wait_recv()

    for k in range(NB // 4):
        tile = zero
        for j in range(4):
            b = 4 * k + j
            moved = pltpu.roll(
                yrecv[owner[b]].astype(F32), lax.rem(j - position[b] + 4, 4) * 32, 1
            )
            tile = jnp.where(group32 == j, moved, tile)
        old = wrow[:, 128 * k : 128 * (k + 1)]
        new = old - learn_rate * (tile + decay_rate * old)
        wbuf[d, :, 128 * k : 128 * (k + 1)] = new.astype(BF16)

    eye = jnp.where(
        lax.broadcasted_iota(jnp.int32, (128, 128), 0)
        == lax.broadcasted_iota(jnp.int32, (128, 128), 1),
        1.0,
        0.0,
    ).astype(BF16)
    final = PlaneGather(wbuf, wssem, wrsem, x, y)
    final.along_x(0)
    final.along_y()

    for i in range(1, 8):
        final.along_x(i)
        if i > 1:
            final.onward(i - 2)
    final.onward(6)
    final.onward(7)

    pick = jnp.where(
        lax.broadcasted_iota(jnp.int32, (R, 128), 1)
        == lax.broadcasted_iota(jnp.int32, (R, 128), 0) + 16 * m,
        1.0,
        0.0,
    ).astype(BF16)
    tile_start = pl.multiple_of(128 * (d // 8), 128)
    loads[5].wait()
    for s in range(NS):
        part = gbuf[:, s, :, pl.ds(tile_start, 128)].reshape(N, 128)
        columns = dot_nt(pick, part).astype(BF16)
        product = dot_nn(columns, whole(s))
        rg[s] = beta_gram * rg[s] + gram_scale * product
    copy = pltpu.make_async_copy(rg, nr_hbm, osem.at[3])
    copy.start()
    stores.append(copy)

    for dx in (0, 1, 3, 2):
        group = lax.rem(x + dx, NX)
        if dx == 2:
            final.last()
        rows = pl.ds(pl.multiple_of(NY * group, NY), NY)
        columns = pl.ds(pl.multiple_of(128 * group, 128), 128)
        for k in range(NB // 4):
            part = wbuf[rows, :, 128 * k : 128 * (k + 1)].reshape(128, 128)
            out_w[128 * k : 128 * (k + 1), columns] = dot_nt(eye, part).astype(BF16)
        copy = pltpu.make_async_copy(out_w.at[:, columns], w_hbm.at[:, columns], osem.at[4 + dx])
        copy.start()
        stores.append(copy)

    for args in (
        ("dp", ND, d, hsend, hrecv, hssem, hrsem),
        ("dp", ND, d, rsend, rrecv, rssem, rrsem),
        ("dp", ND, d, bsend, brecv, bssem, brsem),
        ("dp", ND, d, usend, urecv, ussem, ursem),
        ("tensor", NT, t, zsend, zrecv, zssem, zrsem),
        ("tensor", NT, t, ysend, yrecv, yssem, yrsem),
    ):
        all_of(*args).wait_send()
    gather.finish()
    final.finish()
    for copy in stores:
        copy.wait()


def hand_over(
    w, nl, nr, nm1, nm2, w_out, nl_out, nr_out, nm1_out, nm2_out, w_v, nl_v, nr_v, nm1_v, nm2_v, sem
):
    triples = []
    for k in range(4):
        part = pl.ds(NB * C // 4 * k, NB * C // 4)
        triples.append((w.at[part], w_v.at[part], w_out.at[part]))
    triples += [(nl, nl_v, nl_out), (nr, nr_v, nr_out), (nm1, nm1_v, nm1_out), (nm2, nm2_v, nm2_out)]
    reads = [pltpu.make_async_copy(a, b, sem.at[0, i]) for i, (a, b, _) in enumerate(triples)]
    writes = [pltpu.make_async_copy(b, c, sem.at[1, i]) for i, (_, b, c) in enumerate(triples)]
    for copy in reads:
        copy.start()
    for read, write in zip(reads, writes):
        read.wait()
        write.start()
    for copy in writes:
        copy.wait()


def per_device(gradient, weight, owner_map, ql, qr, lg, rg, m1, m2):
    vmem = pl.BlockSpec(memory_space=pltpu.VMEM)
    anywhere = pl.BlockSpec(memory_space=pl.ANY)
    rows = jax.ShapeDtypeStruct((NS, R, N), F32)
    dma = pltpu.SemaphoreType.DMA
    outs = pl.pallas_call(
        kernel,
        out_shape=(jax.ShapeDtypeStruct((NB * C, N), BF16), rows, rows, rows, rows),
        in_specs=[pl.BlockSpec(memory_space=pltpu.SMEM), vmem, vmem] + [anywhere] * 6,
        out_specs=(anywhere,) * 5,
        scratch_shapes=[
            pltpu.VMEM((NB * C, N), BF16),
            pltpu.VMEM((NS, N, N), BF16),
            pltpu.VMEM((NS, N, N), BF16),
            pltpu.VMEM((NS, R, N), F32),
            pltpu.VMEM((NS, R, N), F32),
            pltpu.VMEM((NS, R, N), F32),
            pltpu.VMEM((NS, R, N), F32),
            pltpu.VMEM((NB * R, 128), F32),
            pltpu.VMEM((R, NB * C), F32),
            pltpu.VMEM((NT, R, 128), BF16),
            pltpu.VMEM((NT, R, 128), BF16),
            pltpu.VMEM((ND, NS, R, N), BF16),
            pltpu.VMEM((128, N), F32),
            pltpu.VMEM((ND, R, 128), BF16),
            pltpu.VMEM((ND, R, 128), BF16),
            pltpu.VMEM((ND, R, 128), BF16),
            pltpu.VMEM((ND, R, 128), BF16),
            pltpu.VMEM((NS, 128, N), BF16),
            pltpu.VMEM((ND, R, 128), BF16),
            pltpu.VMEM((ND, R, 128), BF16),
            pltpu.VMEM((NS, 128, N), BF16),
            pltpu.VMEM((ND, R, 128), BF16),
            pltpu.VMEM((ND, R, 128), BF16),
            pltpu.VMEM((NT, R, 128), BF16),
            pltpu.VMEM((NT, R, 128), BF16),
            pltpu.VMEM((ND, R, NB * C), BF16),
            dma((6,)),
            dma((8,)),
            dma((1,)),
            dma((1,)),
            dma((1,)),
            dma((ND,)),
            dma((1,)),
            dma((1,)),
            dma((1,)),
            dma((1,)),
            dma((1,)),
            dma((1,)),
            dma((1,)),
            dma((1,)),
            dma((1,)),
            dma((1,)),
            dma((1,)),
            dma((ND,)),
        ],
        compiler_params=pltpu.CompilerParams(
            collective_id=0, has_side_effects=True, vmem_limit_bytes=VMEM_LIMIT
        ),
        name="soap_step",
    )(owner_map.reshape(NB), gradient, weight, ql, qr, lg, rg, m1, m2)
    outs = pl.pallas_call(
        hand_over,
        out_shape=(jax.ShapeDtypeStruct((NB * C, N), BF16), rows, rows, rows, rows),
        in_specs=[anywhere] * 5,
        out_specs=(anywhere,) * 5,
        scratch_shapes=[pltpu.VMEM((NB * C, N), BF16)]
        + [pltpu.VMEM((NS, R, N), F32)] * 4
        + [dma((2, 8))],
        compiler_params=pltpu.CompilerParams(vmem_limit_bytes=VMEM_LIMIT),
        name="hand_over",
    )(*outs)
    new_weight = jnp.transpose(outs[0].reshape(NB, C, N), (0, 2, 1))
    return (new_weight,) + tuple(outs[1:])


def solution(mesh):
    in_specs = (
        P(None, "dp", "tensor"),
        P(None, "dp", "tensor"),
        P(),
        P("tensor", None, None),
        P("tensor", None, None),
        P("tensor", "dp", None),
        P("tensor", "dp", None),
        P("tensor", "dp", None),
        P("tensor", "dp", None),
    )
    out_specs = (
        P(None, None, "tensor"),
        P("tensor", "dp", None),
        P("tensor", "dp", None),
        P("tensor", "dp", None),
        P("tensor", "dp", None),
    )
    return jax.shard_map(
        per_device, mesh=mesh, in_specs=in_specs, out_specs=out_specs, check_vma=False
    )
```

```python
import jax
import jax.numpy as jnp
from jax import lax
from jax.experimental import pallas as pl
from jax.experimental.pallas import tpu as pltpu
from jax.sharding import PartitionSpec as P

beta_one = 0.9
beta_two = 0.999
beta_gram = 0.95
epsilon = 1e-08
learn_rate = 0.01
decay_rate = 0.1

MESH = pl.DeviceIdType.MESH
F32 = jnp.float32
BF16 = jnp.bfloat16

NX = 4
NY = 8
ND = NX * NY
NT = 16
NB = 24
NS = 3
N = 512
R = 16
C = 32
VMEM_LIMIT = 56 * 1024 * 1024


def dot_nt(a, b):
    return lax.dot_general(a, b, (((1,), (1,)), ((), ())), preferred_element_type=F32)


def dot_nn(a, b):
    return lax.dot_general(a, b, (((1,), (0,)), ((), ())), preferred_element_type=F32)


class PlaneGather:
    legs = (1, -1, 2, -2, 3, -3, 4)

    def __init__(self, buf, ssem, rsem, xs, ys):
        self.buf, self.ssem, self.rsem, self.xs, self.ys = buf, ssem, rsem, xs, ys
        self.started = []

    def place(self, dx, dy):
        return self.xs[dx % NX] + self.ys[dy % NY]

    def copy_of(self, dx, dy, tx, ty):
        src = self.place(dx, dy)
        return pltpu.make_async_remote_copy(
            src_ref=self.buf.at[src],
            dst_ref=self.buf.at[src],
            send_sem=self.ssem.at[0],
            recv_sem=self.rsem.at[src],
            device_id={"dp": self.place(tx, ty)},
            device_id_type=MESH,
        )

    def send(self, dx, dy, tx, ty):
        copy = self.copy_of(dx, dy, tx, ty)
        copy.start()
        self.started.append(copy)

    def arrive(self, dx, dy):
        src = self.place(dx, dy)
        pltpu.make_async_remote_copy(
            src_ref=self.buf.at[src],
            dst_ref=self.buf.at[src],
            send_sem=self.ssem.at[0],
            recv_sem=self.rsem.at[src],
            device_id={"dp": self.place(1, 0)},
            device_id_type=MESH,
        ).wait_recv()

    def along_y(self):
        for dy in self.legs:
            self.send(0, 0, 0, dy)

    def begin(self):
        for tx, ty in ((0, 1), (0, -1), (1, 0), (-1, 0)):
            self.send(0, 0, tx, ty)

    def ring(self, k):
        for dy, ty, end in ((-k, 1, 4), (k, -1, 3)):
            if k <= end:
                self.arrive(0, dy)
                if k < end:
                    self.send(0, dy, 0, ty)
                self.send(0, dy, 1, 0)
                self.send(0, dy, -1, 0)

    def along_x(self, i):
        dy = 0
        if i > 0:
            dy = -self.legs[i - 1]
            self.arrive(0, dy)
        self.send(0, dy, 1, 0)
        self.send(0, dy, -1, 0)

    def onward(self, i):
        dy = 0 if i == 0 else -self.legs[i - 1]
        self.arrive(-1, dy)
        self.arrive(1, dy)
        if i % 2 == 0:
            self.send(-1, dy, 1, 0)
        else:
            self.send(1, dy, -1, 0)

    def finish(self):
        chunks = self.buf.at[pl.ds(0, len(self.started))]
        pltpu.make_async_remote_copy(
            src_ref=chunks,
            dst_ref=chunks,
            send_sem=self.ssem.at[0],
            recv_sem=self.rsem.at[0],
            device_id={"dp": self.place(1, 0)},
            device_id_type=MESH,
        ).wait_send()

    def last(self):
        for dy in (0,) + tuple(-k for k in self.legs):
            self.arrive(2, dy)


def kernel(
    own,
    grad,
    weight,
    ql_hbm,
    qr_hbm,
    lg_hbm,
    rg_hbm,
    m1_hbm,
    m2_hbm,
    w_hbm,
    nl_hbm,
    nr_hbm,
    nm1_hbm,
    nm2_hbm,
    out_w,
    ql,
    qr,
    lg,
    rg,
    m1,
    m2,
    wide,
    wrow,
    zsend,
    zrecv,
    gbuf,
    tall,
    hsend,
    hrecv,
    rsend,
    rrecv,
    dpad,
    bsend,
    brecv,
    vpad,
    usend,
    urecv,
    ysend,
    yrecv,
    wbuf,
    lsem,
    osem,
    zssem,
    zrsem,
    gssem,
    grsem,
    hssem,
    hrsem,
    rssem,
    rrsem,
    bssem,
    brsem,
    ussem,
    ursem,
    yssem,
    yrsem,
    wssem,
    wrsem,
):
    d = lax.axis_index("dp")
    t = lax.axis_index("tensor")
    x = d // NY
    y = lax.rem(d, NY)
    xs = [lax.rem(x + k, NX) * NY for k in range(NX)]
    ys = [lax.rem(y + k, NY) for k in range(NY)]

    barrier = pltpu.get_barrier_semaphore()
    for k in range(1, NT):
        pl.semaphore_signal(
            barrier, inc=1, device_id={"tensor": lax.rem(t + k, NT)}, device_id_type=MESH
        )
    for k in range(1, ND):
        pl.semaphore_signal(
            barrier, inc=1, device_id={"dp": xs[k // NY] + ys[k % NY]}, device_id_type=MESH
        )

    def exchange(src, dst, ssem, rsem):
        for dx in (2, 1, 3, 0):
            for dy in (4, 3, 5, 2, 6, 1, 7, 0):
                if dx == 0 and dy == 0:
                    continue
                to = xs[dx] + ys[dy]
                copy = pltpu.make_async_remote_copy(
                    src_ref=src.at[to],
                    dst_ref=dst.at[d],
                    send_sem=ssem.at[0],
                    recv_sem=rsem.at[0],
                    device_id={"dp": to},
                    device_id_type=MESH,
                )
                copy.start()
        dst[d] = src[d]

    def all_of(axis, size, me, src, dst, ssem, rsem):
        return pltpu.make_async_remote_copy(
            src_ref=src.at[pl.ds(0, size - 1)],
            dst_ref=dst.at[pl.ds(0, size - 1)],
            send_sem=ssem.at[0],
            recv_sem=rsem.at[0],
            device_id={axis: lax.rem(me + 1, size)},
            device_id_type=MESH,
        )

    def received(src, dst, ssem, rsem):
        all_of("dp", ND, d, src, dst, ssem, rsem).wait_recv()

    loads = []
    for i, (src, dst) in enumerate(
        ((ql_hbm, ql), (qr_hbm, qr), (m1_hbm, m1), (m2_hbm, m2), (lg_hbm, lg), (rg_hbm, rg))
    ):
        copy = pltpu.make_async_copy(src, dst, lsem.at[i])
        copy.start()
        loads.append(copy)

    owner = [own[b] for b in range(NB)]
    position = []
    for b in range(NB):
        before = jnp.int32(0)
        for b2 in range(b):
            before = before + (owner[b2] == owner[b]).astype(jnp.int32)
        position.append(before)

    lane = lax.broadcasted_iota(jnp.int32, (C, 128), 1)
    row = lax.broadcasted_iota(jnp.int32, (C, 128), 0)
    repeat = jnp.where(lax.rem(lane, C) == row, 1.0, 0.0).astype(BF16)
    wide[...] = dot_nn(grad[...].reshape(NB * R, C), repeat)
    group32 = lax.broadcasted_iota(jnp.int32, (R, 128), 1) // 32
    group16 = lax.broadcasted_iota(jnp.int32, (R, 128), 1) // 16
    zero = jnp.zeros((R, 128), F32)

    u = lax.rem(t, 4)
    place = [lax.rem(u + position[b], 4) for b in range(NB)]
    for o in range(NT):
        tile = zero
        for b in range(NB):
            chosen = jnp.where(owner[b] == o, place[b], -1)
            tile = jnp.where(group32 == chosen, wide[b * R : (b + 1) * R, :], tile)
        zsend[o] = tile.astype(BF16)

    pl.semaphore_wait(barrier, NT - 1 + ND - 1)

    for k in range(1, NT):
        o = lax.rem(t + k, NT)
        copy = pltpu.make_async_remote_copy(
            src_ref=zsend.at[o],
            dst_ref=zrecv.at[t],
            send_sem=zssem.at[0],
            recv_sem=zrsem.at[0],
            device_id={"tensor": o},
            device_id_type=MESH,
        )
        copy.start()
    zrecv[t] = zsend[t]

    wwide = dot_nn(weight[...].reshape(NB * R, C), repeat)
    for k in range(NB // 4):
        tile = zero
        for j in range(4):
            b = 4 * k + j
            tile = jnp.where(group32 == j, wwide[b * R : (b + 1) * R, :], tile)
        wrow[:, 128 * k : 128 * (k + 1)] = tile
    tall[...] = jnp.zeros((128, N), F32)
    for s in range(NS):
        dpad[s] = jnp.zeros((128, N), BF16)
        vpad[s] = jnp.zeros((128, N), BF16)

    all_of("tensor", NT, t, zsend, zrecv, zssem, zrsem).wait_recv()

    for k in range(4):
        tiles = [zrecv[4 * k + j].astype(F32) for j in range(4)]
        for s in range(NS):
            tile = zero
            for j in range(4):
                tile = jnp.where(group32 == (j + s) % 4, tiles[j], tile)
            if s:
                tile = pltpu.roll(tile, 128 - 32 * s, 1)
            gbuf[d, s, :, 128 * k : 128 * (k + 1)] = tile.astype(BF16)

    gather = PlaneGather(gbuf, gssem, grsem, xs, ys)
    m = lax.rem(d, 8)
    h = lax.rem(d, 2)

    def lane_groups(src, offset):
        parts = []
        for k in range(4):
            tile = zero
            for j in range(8):
                tile = jnp.where(group16 == (j + offset) % 8, src[8 * k + j].astype(F32), tile)
            if offset:
                tile = pltpu.roll(tile, 128 - 16 * offset, 1)
            parts.append(tile)
        return jnp.concatenate(parts, axis=1)

    half16 = lax.broadcasted_iota(jnp.int32, (R // 2, 128), 1) // 16

    def fold(turned):
        tiles = turned.reshape(ND, R, 128)
        low = pltpu.roll(tiles[:, R // 2 :].reshape(ND * R // 2, 128), 48, 1)
        folded = tiles[:, : R // 2].reshape(ND * R // 2, 128) + low
        return folded.astype(BF16).reshape(ND, R // 2, 128)

    def unfold(src, offset):
        parts = []
        for k in range(4):
            halves = []
            for shift in (offset, offset + 3):
                tile = jnp.zeros((R // 2, 128), F32)
                for j in range(8):
                    chosen = half16 == (j + shift) % 8
                    tile = jnp.where(chosen, src[8 * k + j].astype(F32), tile)
                if shift:
                    tile = pltpu.roll(tile, 128 - 16 * shift, 1)
                halves.append(tile)
            parts.append(jnp.concatenate(halves, axis=0))
        return jnp.concatenate(parts, axis=1)

    def group_at(offset):
        return pl.ds(pl.multiple_of(16 * lax.rem(m + offset, 8), 16), 16)

    loads[1].wait()
    for s in range(NS):
        tall[group_at(s), :] = dot_nn(gbuf[d, s], qr[s])
    hsend[...] = fold(tall[...].T)
    exchange(hsend, hrecv, hssem, hrsem)
    gather.begin()
    gather.ring(1)

    loads[0].wait()
    received(hsend, hrecv, hssem, hrsem)
    for s in range(NS):
        half = unfold(hrecv, s).astype(BF16)
        turned = dot_nn(half, ql[s])
        high = turned.astype(BF16).astype(F32)
        tall[group_at(s), :] = high
        tall[group_at(s + 3), :] = turned - high
    rsend[...] = tall[...].T.astype(BF16).reshape(ND, R, 128)
    exchange(rsend, rrecv, rssem, rrsem)
    gather.ring(2)
    gather.ring(3)

    for i in range(2, 4):
        loads[i].wait()
    received(rsend, rrecv, rssem, rrsem)
    stores = []
    for s in range(NS):
        rotated = lane_groups(rrecv, s) + lane_groups(rrecv, s + 3)
        first = beta_one * m1[s] + (1.0 - beta_one) * rotated
        second = beta_two * m2[s] + (1.0 - beta_two) * rotated * rotated
        m1[s] = first
        m2[s] = second
        direction = (first / (jnp.sqrt(second) + epsilon)).astype(BF16)
        dpad[s, group_at(s), :] = direction
    for i, (src, dst) in enumerate(((m1, nm1_hbm), (m2, nm2_hbm))):
        copy = pltpu.make_async_copy(src, dst, osem.at[i])
        copy.start()
        stores.append(copy)

    turned = dot_nt(qr[0], dpad[0])
    for s in range(1, NS):
        turned = turned + dot_nt(qr[s], dpad[s])
    bsend[...] = fold(turned)

    exchange(bsend, brecv, bssem, brsem)

    gather.ring(4)
    for i in range(4):
        gather.onward(i)

    received(bsend, brecv, bssem, brsem)

    for s in range(NS):
        at = pl.multiple_of(32 * s + 16 * h, 16)
        vpad[s, pl.ds(at, 16), :] = unfold(brecv, s).astype(BF16)
    update = dot_nt(ql[0], vpad[0])
    for s in range(1, NS):
        update = update + dot_nt(ql[s], vpad[s])
    usend[...] = update.astype(BF16).reshape(ND, R, 128)
    exchange(usend, urecv, ussem, ursem)

    for i in range(4, 8):
        gather.onward(i)

    received(usend, urecv, ussem, ursem)

    for o in range(NT):
        ysend[o] = (urecv[2 * o].astype(F32) + urecv[2 * o + 1].astype(F32)).astype(BF16)
    for k in range(1, NT):
        o = lax.rem(t + k, NT)
        copy = pltpu.make_async_remote_copy(
            src_ref=ysend.at[o],
            dst_ref=yrecv.at[t],
            send_sem=yssem.at[0],
            recv_sem=yrsem.at[0],
            device_id={"tensor": o},
            device_id_type=MESH,
        )
        copy.start()
    yrecv[t] = ysend[t]

    def whole(s):
        return gbuf[:, s].reshape(N, N)

    gather.last()
    gram_scale = 1.0 - beta_gram
    loads[4].wait()
    for s in range(NS):
        product = dot_nt(gbuf[d, s], whole(s))
        lg[s] = beta_gram * lg[s] + gram_scale * product
    copy = pltpu.make_async_copy(lg, nl_hbm, osem.at[2])
    copy.start()
    stores.append(copy)

    all_of("tensor", NT, t, ysend, yrecv, yssem, yrsem).wait_recv()

    for k in range(NB // 4):
        tile = zero
        for j in range(4):
            b = 4 * k + j
            moved = pltpu.roll(
                yrecv[owner[b]].astype(F32), lax.rem(j - position[b] + 4, 4) * 32, 1
            )
            tile = jnp.where(group32 == j, moved, tile)
        old = wrow[:, 128 * k : 128 * (k + 1)]
        new = old - learn_rate * (tile + decay_rate * old)
        wbuf[d, :, 128 * k : 128 * (k + 1)] = new.astype(BF16)

    eye = jnp.where(
        lax.broadcasted_iota(jnp.int32, (128, 128), 0)
        == lax.broadcasted_iota(jnp.int32, (128, 128), 1),
        1.0,
        0.0,
    ).astype(BF16)
    final = PlaneGather(wbuf, wssem, wrsem, xs, ys)
    final.along_x(0)
    final.along_y()

    for i in range(1, 8):
        final.along_x(i)
        if i > 1:
            final.onward(i - 2)
    final.onward(6)
    final.onward(7)

    pick = jnp.where(
        lax.broadcasted_iota(jnp.int32, (R, 128), 1)
        == lax.broadcasted_iota(jnp.int32, (R, 128), 0) + 16 * m,
        1.0,
        0.0,
    ).astype(BF16)
    tile_start = pl.multiple_of(128 * (d // 8), 128)
    loads[5].wait()
    for s in range(NS):
        part = gbuf[:, s, :, pl.ds(tile_start, 128)].reshape(N, 128)
        columns = dot_nt(pick, part).astype(BF16)
        product = dot_nn(columns, whole(s))
        rg[s] = beta_gram * rg[s] + gram_scale * product
    copy = pltpu.make_async_copy(rg, nr_hbm, osem.at[3])
    copy.start()
    stores.append(copy)

    for dx in (0, 1, 3, 2):
        group = lax.rem(x + dx, NX)
        if dx == 2:
            final.last()
        rows = pl.ds(pl.multiple_of(NY * group, NY), NY)
        columns = pl.ds(pl.multiple_of(128 * group, 128), 128)
        for k in range(NB // 4):
            part = wbuf[rows, :, 128 * k : 128 * (k + 1)].reshape(128, 128)
            out_w[128 * k : 128 * (k + 1), columns] = dot_nt(eye, part).astype(BF16)
        copy = pltpu.make_async_copy(out_w.at[:, columns], w_hbm.at[:, columns], osem.at[4 + dx])
        copy.start()
        stores.append(copy)

    for args in (
        ("dp", ND, d, hsend, hrecv, hssem, hrsem),
        ("dp", ND, d, rsend, rrecv, rssem, rrsem),
        ("dp", ND, d, bsend, brecv, bssem, brsem),
        ("dp", ND, d, usend, urecv, ussem, ursem),
        ("tensor", NT, t, zsend, zrecv, zssem, zrsem),
        ("tensor", NT, t, ysend, yrecv, yssem, yrsem),
    ):
        all_of(*args).wait_send()
    gather.finish()
    final.finish()
    for copy in stores:
        copy.wait()


def hand_over(
    w, nl, nr, nm1, nm2, w_out, nl_out, nr_out, nm1_out, nm2_out, w_v, nl_v, nr_v, nm1_v, nm2_v, sem
):
    triples = []
    for k in range(4):
        part = pl.ds(NB * C // 4 * k, NB * C // 4)
        triples.append((w.at[part], w_v.at[part], w_out.at[part]))
    triples += [(nl, nl_v, nl_out), (nr, nr_v, nr_out), (nm1, nm1_v, nm1_out), (nm2, nm2_v, nm2_out)]
    reads = [pltpu.make_async_copy(a, b, sem.at[0, i]) for i, (a, b, _) in enumerate(triples)]
    writes = [pltpu.make_async_copy(b, c, sem.at[1, i]) for i, (_, b, c) in enumerate(triples)]
    for copy in reads:
        copy.start()
    for read, write in zip(reads, writes):
        read.wait()
        write.start()
    for copy in writes:
        copy.wait()


def per_device(gradient, weight, owner_map, ql, qr, lg, rg, m1, m2):
    vmem = pl.BlockSpec(memory_space=pltpu.VMEM)
    anywhere = pl.BlockSpec(memory_space=pl.ANY)
    rows = jax.ShapeDtypeStruct((NS, R, N), F32)
    dma = pltpu.SemaphoreType.DMA
    outs = pl.pallas_call(
        kernel,
        out_shape=(jax.ShapeDtypeStruct((NB * C, N), BF16), rows, rows, rows, rows),
        in_specs=[pl.BlockSpec(memory_space=pltpu.SMEM), vmem, vmem] + [anywhere] * 6,
        out_specs=(anywhere,) * 5,
        scratch_shapes=[
            pltpu.VMEM((NB * C, N), BF16),
            pltpu.VMEM((NS, N, N), BF16),
            pltpu.VMEM((NS, N, N), BF16),
            pltpu.VMEM((NS, R, N), F32),
            pltpu.VMEM((NS, R, N), F32),
            pltpu.VMEM((NS, R, N), F32),
            pltpu.VMEM((NS, R, N), F32),
            pltpu.VMEM((NB * R, 128), F32),
            pltpu.VMEM((R, NB * C), F32),
            pltpu.VMEM((NT, R, 128), BF16),
            pltpu.VMEM((NT, R, 128), BF16),
            pltpu.VMEM((ND, NS, R, N), BF16),
            pltpu.VMEM((128, N), F32),
            pltpu.VMEM((ND, R // 2, 128), BF16),
            pltpu.VMEM((ND, R // 2, 128), BF16),
            pltpu.VMEM((ND, R, 128), BF16),
            pltpu.VMEM((ND, R, 128), BF16),
            pltpu.VMEM((NS, 128, N), BF16),
            pltpu.VMEM((ND, R // 2, 128), BF16),
            pltpu.VMEM((ND, R // 2, 128), BF16),
            pltpu.VMEM((NS, 128, N), BF16),
            pltpu.VMEM((ND, R, 128), BF16),
            pltpu.VMEM((ND, R, 128), BF16),
            pltpu.VMEM((NT, R, 128), BF16),
            pltpu.VMEM((NT, R, 128), BF16),
            pltpu.VMEM((ND, R, NB * C), BF16),
            dma((6,)),
            dma((8,)),
            dma((1,)),
            dma((1,)),
            dma((1,)),
            dma((ND,)),
            dma((1,)),
            dma((1,)),
            dma((1,)),
            dma((1,)),
            dma((1,)),
            dma((1,)),
            dma((1,)),
            dma((1,)),
            dma((1,)),
            dma((1,)),
            dma((1,)),
            dma((ND,)),
        ],
        compiler_params=pltpu.CompilerParams(
            collective_id=0, has_side_effects=True, vmem_limit_bytes=VMEM_LIMIT
        ),
        name="soap_step",
    )(owner_map.reshape(NB), gradient, weight, ql, qr, lg, rg, m1, m2)
    outs = pl.pallas_call(
        hand_over,
        out_shape=(jax.ShapeDtypeStruct((NB * C, N), BF16), rows, rows, rows, rows),
        in_specs=[anywhere] * 5,
        out_specs=(anywhere,) * 5,
        scratch_shapes=[pltpu.VMEM((NB * C, N), BF16)]
        + [pltpu.VMEM((NS, R, N), F32)] * 4
        + [dma((2, 8))],
        compiler_params=pltpu.CompilerParams(vmem_limit_bytes=VMEM_LIMIT),
        name="hand_over",
    )(*outs)
    new_weight = jnp.transpose(outs[0].reshape(NB, C, N), (0, 2, 1))
    return (new_weight,) + tuple(outs[1:])


def solution(mesh):
    in_specs = (
        P(None, "dp", "tensor"),
        P(None, "dp", "tensor"),
        P(),
        P("tensor", None, None),
        P("tensor", None, None),
        P("tensor", "dp", None),
        P("tensor", "dp", None),
        P("tensor", "dp", None),
        P("tensor", "dp", None),
    )
    out_specs = (
        P(None, None, "tensor"),
        P("tensor", "dp", None),
        P("tensor", "dp", None),
        P("tensor", "dp", None),
        P("tensor", "dp", None),
    )
    return jax.shard_map(
        per_device, mesh=mesh, in_specs=in_specs, out_specs=out_specs, check_vma=False
    )
```
